128 devices in a mesh: seq: 32 (over x, z_hi, y), dp: 4 (over z_lo, core).
Axes of the slice: x: 4, y: 4, z: 4 (z_hi: 2, z_lo: 2; z = z_hi * 2 + z_lo), core: 2. Of those that a mesh axis runs over, the one named last changes fastest.
Arguments:
- tokens: bfloat16 [4, 32, 384, 1152], P('dp', 'seq'), may hold values from -6 to 6
- cotangent: bfloat16 [4, 32, 384, 1152], P('dp', 'seq'), may hold values from -6 to 6
- mask: int32 [4, 32, 384], P('dp'), may hold values 0 or 1
- t_index: int32 [4], P('dp'), may hold values from 1 to 15
- mod_table: float32 [16, 6, 1152], replicated, may hold values from -3 to 3
- wqkv_s: bfloat16 [1152, 1728], replicated
- wo_s: bfloat16 [576, 1152], replicated, may hold values from -0.25 to 0.25
- wqkv_t: bfloat16 [1152, 1728], replicated
- wo_t: bfloat16 [576, 1152], replicated, may hold values from -0.25 to 0.25
Outputs:
- grad_tokens: float32 [4, 32, 384, 1152], P('dp', 'seq')
- grad_wqkv_s: float32 [1152, 1728], P('seq')
- grad_wo_s: float32 [576, 1152], P('seq')
- grad_wqkv_t: float32 [1152, 1728], P('seq')
- grad_wo_t: float32 [576, 1152], P('seq')
The draws below stay inside these ranges and needn't reach their ends.
All inputs are finite; a program needn't handle non-finite values. No bound on the sum of `mask` on one device may be relied on, other than what follows from the above.
Results may differ from the reference program's by a relative error of at most 0.039.
The reference program's roundings to bfloat16 on the way count: a program that leaves them out, or rounds other values in their place, can miss the bound.
Values may be sent and summed in bfloat16 or wider, within the bound.
No kernel may reach another device: no remote copies, remote signals or barrier semaphores. Data moves between devices by JAX's collectives and lax.ppermute only.
A program may use at most 128 MiB of HBM per device.

```python
import math
import jax
import jax.numpy as jnp
from jax import lax

D = 1152
H = 8
E = 72
HD = 576
P_SIZE = 384
FRAMES = 32
CLIPS = 4
NT = 16


def projection_draw(key):
    width = H * E
    base = jax.random.normal(key, (D, 3 * width), jnp.float32) * D ** (-0.5)
    return base.astype(jnp.bfloat16)


def draw_wqkv_s(key, part):
    key = jax.random.fold_in(key, 11)
    return projection_draw(key)


def draw_wqkv_t(key, part):
    key = jax.random.fold_in(key, 23)
    return projection_draw(key)


def with_ends(array, key, smallest, high):
    place = [jax.random.randint(jax.random.fold_in(key, axis), (), 0, length) for axis, length in enumerate(array.shape)]
    main_axis = array.shape.index(max(array.shape))
    beside = place[:main_axis] + [(place[main_axis] + 1) % array.shape[main_axis]] + place[main_axis + 1:]
    return array.at[tuple(place)].set(smallest).at[tuple(beside)].set(high)


def shard_levels(rng, dims, pieces, least, largest):
    gain, own = 1.0, jax.random.fold_in(rng, 6)
    for dim, blocks in pieces:
        steps = jnp.exp(jax.random.uniform(jax.random.fold_in(own, dim), (blocks,), jnp.float32, least / len(pieces), largest / len(pieces)))
        gain = gain * jnp.repeat(steps, dims[dim] // blocks).reshape([-1 if axis == dim else 1 for axis in range(len(dims))])
    return gain


def centred(stream_key, dims, spread, bound, split=(), kind=jnp.bfloat16):
    drawn = spread * jax.random.normal(stream_key, dims, jnp.float32)
    if split:
        drawn = drawn * shard_levels(stream_key, dims, split, -0.22, 0.18)
    return jnp.clip(drawn, -bound, bound).astype(kind)


def setup_inputs(seed: int = 0) -> dict:
    arg_keys = jax.random.split(jax.random.key(seed), 10)
    tokens = centred(arg_keys[0], (CLIPS, FRAMES, P_SIZE, D), 1.0, 6.0, ((0, 4), (1, 32)))
    cotangent = centred(arg_keys[1], (CLIPS, FRAMES, P_SIZE, D), 1.0, 6.0, ((0, 4), (1, 32)))
    mask = with_ends((jax.random.randint(arg_keys[2], (CLIPS, FRAMES, P_SIZE), 0, 2) < 1).astype(jnp.int32), jax.random.fold_in(arg_keys[2], 1), 0, 1)
    t_index = with_ends(jax.random.randint(arg_keys[3], (CLIPS,), 1, NT), jax.random.fold_in(arg_keys[3], 1), 1, NT - 1).astype(jnp.int32)
    mod_table = centred(arg_keys[4], (NT, 6, D), 0.5, 3.0, (), jnp.float32)
    wqkv_s = draw_wqkv_s(jax.random.fold_in(arg_keys[9], 71), 0)
    wo_s = centred(arg_keys[6], (HD, D), HD ** -0.5, 0.25)
    wqkv_t = draw_wqkv_t(jax.random.fold_in(arg_keys[9], 71), 0)
    wo_t = centred(arg_keys[8], (HD, D), HD ** -0.5, 0.25)
    return dict(tokens=tokens, cotangent=cotangent, mask=mask, t_index=t_index, mod_table=mod_table, wqkv_s=wqkv_s, wo_s=wo_s, wqkv_t=wqkv_t, wo_t=wo_t)


def modulate(marks, row_clean, row_noised, base):
    chosen = (marks == 1)[..., None]
    shift_offset = jnp.where(chosen, row_clean[base], row_noised[base])
    scale_factor = jnp.where(chosen, row_clean[base + 1], row_noised[base + 1])
    gate_factor = jnp.where(chosen, row_clean[base + 2], row_noised[base + 2])
    return (shift_offset, scale_factor, gate_factor)

def softmax_bf(scores):
    top = lax.optimization_barrier(jnp.max(scores, axis=-1, keepdims=True))
    expo = jnp.exp(scores - top)
    probs = expo / lax.optimization_barrier(jnp.sum(expo, axis=-1, keepdims=True))
    return lax.optimization_barrier(probs.astype(jnp.bfloat16)).astype(jnp.float32)

def core_spatial(query_key_value):
    count, length, _ = query_key_value.shape
    width = H * E
    query = query_key_value[..., :width].astype(jnp.float32).reshape(count, length, H, E)
    keys = query_key_value[..., width:2 * width].astype(jnp.float32).reshape(count, length, H, E)
    values = query_key_value[..., 2 * width:].astype(jnp.float32).reshape(count, length, H, E)
    scores = jnp.einsum('nqhe,nkhe->nhqk', query, keys) * E ** (-0.5)
    probs = softmax_bf(scores)
    head_split = jnp.einsum('nhqk,nkhe->nqhe', probs, values)
    return head_split.reshape(count, length, width).astype(jnp.bfloat16)

def core_temporal(query_key_value):
    length, count, _ = query_key_value.shape
    width = H * E
    query = query_key_value[..., :width].astype(jnp.float32).reshape(length, count, H, E)
    keys = query_key_value[..., width:2 * width].astype(jnp.float32).reshape(length, count, H, E)
    values = query_key_value[..., 2 * width:].astype(jnp.float32).reshape(length, count, H, E)
    scores = jnp.einsum('qnhe,knhe->nhqk', query, keys) * E ** (-0.5)
    probs = softmax_bf(scores)
    head_split = jnp.einsum('nhqk,knhe->qnhe', probs, values)
    return head_split.reshape(length, count, width).astype(jnp.bfloat16)

def branch_forward(inputs, marks, row_clean, row_noised, base, wqkv, wout, core):
    shift_offset, scale_factor, gate_factor = modulate(marks, row_clean, row_noised, base)
    xfull = inputs.astype(jnp.float32)
    centered_input = xfull - lax.optimization_barrier(jnp.mean(xfull, axis=-1, keepdims=True))
    inverse_deviation = lax.rsqrt(lax.optimization_barrier(jnp.mean(centered_input * centered_input, axis=-1, keepdims=True)) + 1e-06)
    normalized_input = centered_input * inverse_deviation
    norm_output = (normalized_input * (1.0 + scale_factor) + shift_offset).astype(jnp.bfloat16)
    query_key_value = jnp.dot(norm_output, wqkv, preferred_element_type=jnp.float32).astype(jnp.bfloat16)
    head_split = core(query_key_value)
    attn = jnp.dot(head_split, wout, preferred_element_type=jnp.float32)
    output_rows = (xfull + gate_factor * attn).astype(jnp.bfloat16)
    return (output_rows, (normalized_input, inverse_deviation, norm_output, query_key_value, head_split, gate_factor, scale_factor))

def branch_backward(saved_residuals, wqkv, wout, core, dout):
    normalized_input, inverse_deviation, norm_output, query_key_value, head_split, gate_factor, scale_factor = saved_residuals
    dres = dout.astype(jnp.float32)
    dattn = (dres * gate_factor).astype(jnp.bfloat16)
    width = head_split.shape[-1]
    g_wo = lax.dot_general(head_split.reshape(-1, width), dattn.reshape(-1, dattn.shape[-1]), (((0,), (0,)), ((), ())), preferred_element_type=jnp.float32)
    last = dattn.ndim - 1
    dheads = lax.dot_general(dattn, wout, (((last,), (1,)), ((), ())), preferred_element_type=jnp.float32).astype(jnp.bfloat16)
    _, pull = jax.vjp(core, query_key_value)
    dqkv = pull(dheads)[0]
    g_wqkv = lax.dot_general(norm_output.reshape(-1, norm_output.shape[-1]), dqkv.reshape(-1, dqkv.shape[-1]), (((0,), (0,)), ((), ())), preferred_element_type=jnp.float32)
    dnormed = lax.dot_general(dqkv, wqkv, (((last,), (1,)), ((), ())), preferred_element_type=jnp.float32)
    normalized_gradient = dnormed * (1.0 + scale_factor)
    line_gradient = inverse_deviation * (normalized_gradient - lax.optimization_barrier(jnp.mean(normalized_gradient, axis=-1, keepdims=True)) - normalized_input * lax.optimization_barrier(jnp.mean(normalized_gradient * normalized_input, axis=-1, keepdims=True)))
    return (dres + line_gradient, g_wqkv, g_wo)

def reference(tokens, cotangent, mask, t_index, mod_table, wqkv_s, wo_s, wqkv_t, wo_t):
    clips, frames, patches, _ = tokens.shape
    totals = [jnp.zeros(wqkv_s.shape, jnp.float32), jnp.zeros(wo_s.shape, jnp.float32), jnp.zeros(wqkv_t.shape, jnp.float32), jnp.zeros(wo_t.shape, jnp.float32)]
    grads_out = []
    for clip in range(clips):
        row_clean = mod_table[0]
        row_noised = mod_table[t_index[clip]]

        def frame_forward(pair):
            frame, marks = pair
            output_rows, _ = branch_forward(frame[None], marks[None], row_clean, row_noised, 0, wqkv_s, wo_s, core_spatial)
            return output_rows[0]
        middle = lax.map(frame_forward, (tokens[clip], mask[clip]))
        _, saved_residuals = branch_forward(middle, mask[clip], row_clean, row_noised, 3, wqkv_t, wo_t, core_temporal)
        dmiddle, gq_t, go_t = branch_backward(saved_residuals, wqkv_t, wo_t, core_temporal, cotangent[clip])

        def frame_backward(carry, triple):
            frame, marks, dframe = triple
            _, kept = branch_forward(frame[None], marks[None], row_clean, row_noised, 0, wqkv_s, wo_s, core_spatial)
            dframe_in, gq, go = branch_backward(kept, wqkv_s, wo_s, core_spatial, dframe[None])
            return ((carry[0] + gq, carry[1] + go), dframe_in[0])
        start = (jnp.zeros(wqkv_s.shape, jnp.float32), jnp.zeros(wo_s.shape, jnp.float32))
        (gq_s, go_s), dclip = lax.scan(frame_backward, start, (tokens[clip], mask[clip], dmiddle))
        grads_out.append(dclip)
        totals = [totals[0] + gq_s, totals[1] + go_s, totals[2] + gq_t, totals[3] + go_t]
    factor = 1.0 / math.sqrt(clips * frames * patches)
    return (jnp.stack(grads_out), totals[0] * factor, totals[1] * factor, totals[2] * factor, totals[3] * factor)
```

```python
import math

import jax
import jax.numpy as jnp
from jax import lax
from jax.sharding import PartitionSpec as P

H = 8
E = 72


def modulate(marks, row_clean, row_noised, base):
    chosen = (marks == 1)[..., None]
    shift_offset = jnp.where(chosen, row_clean[base], row_noised[base])
    scale_factor = jnp.where(chosen, row_clean[base + 1], row_noised[base + 1])
    gate_factor = jnp.where(chosen, row_clean[base + 2], row_noised[base + 2])
    return (shift_offset, scale_factor, gate_factor)


def softmax_bf(scores):
    top = jnp.max(scores, axis=-1, keepdims=True)
    expo = jnp.exp(scores - top)
    probs = expo / jnp.sum(expo, axis=-1, keepdims=True)
    return lax.optimization_barrier(probs.astype(jnp.bfloat16)).astype(jnp.float32)


def core_spatial(query_key_value):
    count, length, _ = query_key_value.shape
    width = H * E
    query = query_key_value[..., :width].astype(jnp.float32).reshape(count, length, H, E)
    keys = query_key_value[..., width : 2 * width].astype(jnp.float32).reshape(count, length, H, E)
    values = query_key_value[..., 2 * width :].astype(jnp.float32).reshape(count, length, H, E)
    scores = jnp.einsum("nqhe,nkhe->nhqk", query, keys) * E ** (-0.5)
    probs = softmax_bf(scores)
    head_split = jnp.einsum("nhqk,nkhe->nqhe", probs, values)
    return head_split.reshape(count, length, width).astype(jnp.bfloat16)


def core_temporal(query_key_value):
    length, count, _ = query_key_value.shape
    width = H * E
    query = query_key_value[..., :width].astype(jnp.float32).reshape(length, count, H, E)
    keys = query_key_value[..., width : 2 * width].astype(jnp.float32).reshape(length, count, H, E)
    values = query_key_value[..., 2 * width :].astype(jnp.float32).reshape(length, count, H, E)
    scores = jnp.einsum("qnhe,knhe->nhqk", query, keys) * E ** (-0.5)
    probs = softmax_bf(scores)
    head_split = jnp.einsum("nhqk,knhe->qnhe", probs, values)
    return head_split.reshape(length, count, width).astype(jnp.bfloat16)


def branch_forward(inputs, marks, row_clean, row_noised, base, wqkv, wout, core):
    shift_offset, scale_factor, gate_factor = modulate(marks, row_clean, row_noised, base)
    xfull = inputs.astype(jnp.float32)
    centered_input = xfull - jnp.mean(xfull, axis=-1, keepdims=True)
    inverse_deviation = lax.rsqrt(
        jnp.mean(centered_input * centered_input, axis=-1, keepdims=True) + 1e-06
    )
    normalized_input = centered_input * inverse_deviation
    norm_output = (normalized_input * (1.0 + scale_factor) + shift_offset).astype(jnp.bfloat16)
    query_key_value = jnp.dot(norm_output, wqkv, preferred_element_type=jnp.float32).astype(
        jnp.bfloat16
    )
    head_split = core(query_key_value)
    attn = jnp.dot(head_split, wout, preferred_element_type=jnp.float32)
    output_rows = (xfull + gate_factor * attn).astype(jnp.bfloat16)
    return (
        output_rows,
        (
            normalized_input,
            inverse_deviation,
            norm_output,
            query_key_value,
            head_split,
            gate_factor,
            scale_factor,
        ),
    )


def branch_backward(saved_residuals, wqkv, wout, core, dout):
    (
        normalized_input,
        inverse_deviation,
        norm_output,
        query_key_value,
        head_split,
        gate_factor,
        scale_factor,
    ) = saved_residuals
    dres = dout.astype(jnp.float32)
    dattn = (dres * gate_factor).astype(jnp.bfloat16)
    width = head_split.shape[-1]
    g_wo = lax.dot_general(
        head_split.reshape(-1, width),
        dattn.reshape(-1, dattn.shape[-1]),
        (((0,), (0,)), ((), ())),
        preferred_element_type=jnp.float32,
    )
    last = dattn.ndim - 1
    dheads = lax.dot_general(
        dattn, wout, (((last,), (1,)), ((), ())), preferred_element_type=jnp.float32
    ).astype(jnp.bfloat16)
    _, pull = jax.vjp(core, query_key_value)
    dqkv = pull(dheads)[0]
    g_wqkv = lax.dot_general(
        norm_output.reshape(-1, norm_output.shape[-1]),
        dqkv.reshape(-1, dqkv.shape[-1]),
        (((0,), (0,)), ((), ())),
        preferred_element_type=jnp.float32,
    )
    dnormed = lax.dot_general(
        dqkv, wqkv, (((last,), (1,)), ((), ())), preferred_element_type=jnp.float32
    )
    normalized_gradient = dnormed * (1.0 + scale_factor)
    line_gradient = inverse_deviation * (
        normalized_gradient
        - jnp.mean(normalized_gradient, axis=-1, keepdims=True)
        - normalized_input
        * jnp.mean(normalized_gradient * normalized_input, axis=-1, keepdims=True)
    )
    return (dres + line_gradient, g_wqkv, g_wo)


def body(tokens, cotangent, mask, t_index, mod_table, wqkv_s, wo_s, wqkv_t, wo_t):
    seq_count = lax.axis_size("seq")
    seq_rank = lax.axis_index("seq")
    frame_count = tokens.shape[1]
    patches = tokens.shape[2]
    patch_count = patches // seq_count
    row_clean = mod_table[0]
    row_noised = lax.dynamic_index_in_dim(mod_table, t_index[0], 0, keepdims=False)
    frame_marks = lax.dynamic_slice_in_dim(mask[0], seq_rank * frame_count, frame_count, 0)
    patch_marks = lax.dynamic_slice_in_dim(mask[0], seq_rank * patch_count, patch_count, 1)
    local_frames = tokens[0]
    middle, saved_s = branch_forward(
        local_frames, frame_marks, row_clean, row_noised, 0, wqkv_s, wo_s, core_spatial
    )
    middle_patch, dpatch = (
        lax.all_to_all(middle, "seq", split_axis=1, concat_axis=0, tiled=True),
        lax.all_to_all(cotangent[0], "seq", split_axis=1, concat_axis=0, tiled=True),
    )
    _, saved_t = branch_forward(
        middle_patch, patch_marks, row_clean, row_noised, 3, wqkv_t, wo_t, core_temporal
    )
    dmiddle_patch, gq_t, go_t = branch_backward(saved_t, wqkv_t, wo_t, core_temporal, dpatch)
    dmiddle = lax.all_to_all(
        dmiddle_patch.astype(jnp.bfloat16), "seq", split_axis=0, concat_axis=1, tiled=True
    )
    dlocal, gq_s, go_s = branch_backward(saved_s, wqkv_s, wo_s, core_spatial, dmiddle)
    factor = 1.0 / math.sqrt(lax.axis_size("dp") * frame_count * seq_count * patches)
    gq_t, go_t = reduce_pair(gq_t, go_t, factor)
    gq_s, go_s = reduce_pair(gq_s, go_s, factor)
    return (dlocal[None], gq_s, go_s, gq_t, go_t)


def reduce_pair(gq, go, factor):
    count = lax.axis_size("seq")
    packed = jnp.concatenate(
        [
            gq.astype(jnp.bfloat16).reshape(count, -1, 128),
            go.astype(jnp.bfloat16).reshape(count, -1, 128),
        ],
        axis=1,
    )
    shares = lax.all_to_all(packed, "seq", 0, 0, tiled=True)
    own = jnp.sum(shares.astype(jnp.float32), axis=0)
    total = jnp.sum(lax.all_gather(own, "dp", axis=0), axis=0) * factor
    cut = gq.size // count // 128
    return (
        total[:cut].reshape(gq.shape[0] // count, gq.shape[1]),
        total[cut:].reshape(go.shape[0] // count, go.shape[1]),
    )


def solution(mesh):
    return jax.shard_map(
        body,
        mesh=mesh,
        in_specs=(
            P("dp", "seq", None, None),
            P("dp", "seq", None, None),
            P("dp", None, None),
            P("dp"),
            P(),
            P(),
            P(),
            P(),
            P(),
        ),
        out_specs=(
            P("dp", "seq", None, None),
            P("seq", None),
            P("seq", None),
            P("seq", None),
            P("seq", None),
        ),
        check_vma=False,
    )
```

```python
import math

import jax
import jax.numpy as jnp
from jax import lax
from jax.experimental import pallas as pl
from jax.experimental.pallas import tpu as pltpu
from jax.sharding import PartitionSpec as P

D = 1152
H = 8
E = 72
HD = 576
N = 384
F = 32
W = 640
LATE = 256
REST = 128
PACK = 1792
GQ = 896
GO = 640
ROWS = 352
BF = jnp.bfloat16
F32 = jnp.float32
SCALE = E**-0.5
VMEM = pl.BlockSpec(memory_space=pltpu.VMEM)
SMEM = pl.BlockSpec(memory_space=pltpu.SMEM)


def call(kernel, out, *args, scratch=()):
    return pl.pallas_call(
        kernel,
        out_shape=[jax.ShapeDtypeStruct(shape, kind) for shape, kind in out],
        in_specs=[SMEM] + [VMEM] * (len(args) - 1),
        out_specs=[VMEM] * len(out),
        scratch_shapes=[pltpu.VMEM(shape, kind) for shape, kind in scratch],
        compiler_params=pltpu.CompilerParams(vmem_limit_bytes=56 * 1024 * 1024),
        name=kernel.__name__,
    )(*args)


def nn(a, b):
    return lax.dot_general(a, b, (((1,), (0,)), ((), ())), preferred_element_type=F32)


def nt(a, b):
    return lax.dot_general(a, b, (((1,), (1,)), ((), ())), preferred_element_type=F32)


def tn(a, b):
    return lax.dot_general(a, b, (((0,), (0,)), ((), ())), preferred_element_type=F32)


def iota(shape, dim):
    return lax.broadcasted_iota(jnp.int32, shape, dim)


def one_hot(test):
    return jnp.where(test, 1.0, 0.0).astype(BF)


def rest_pick(back):
    shape = (LATE, 2 * REST)
    row, col = iota(shape, 0), iota(shape, 1)
    if back:
        shape = (2 * REST, LATE)
        row, col = iota(shape, 1), iota(shape, 0)
    return one_hot((row & 3) + 4 * (row >> 3) + REST * ((row >> 2) & 1) == col)


def pack_frame(rows, out_ref):
    out_ref[:, :D] = rows[:LATE]
    low = rows[LATE:, :W]
    high = jnp.concatenate([rows[LATE:, W:], jnp.zeros((REST, 2 * W - D), BF)], axis=1)
    both = jnp.concatenate([low, high], axis=0)
    out_ref[:, D:] = nn(rest_pick(False), both).astype(BF)


def unpack_frame(got_ref):
    both = nn(rest_pick(True), got_ref[:, D:])
    rest = jnp.concatenate([both[:REST], both[REST:, : D - W]], axis=1).astype(BF)
    return got_ref[:, :D], rest


def patch_pick():
    shape = (LATE, LATE)
    row, col = iota(shape, 0), iota(shape, 1)
    return one_hot((row & 31) * 8 + (row >> 5) == col)


def unpack_patches(got_ref, pick):
    first = nn(pick, got_ref[:, :D])
    rest = nn(pick, got_ref[:, D:])
    rest = jnp.concatenate([rest[:REST], rest[REST:, : D - W]], axis=1)
    return jnp.concatenate([first, rest], axis=0).astype(BF)


def pack_patches(rows, pick, out_ref):
    out_ref[:, :D] = tn(pick, rows[:LATE]).astype(BF)
    low = rows[LATE:, :W]
    high = jnp.concatenate([rows[LATE:, W:], jnp.zeros((REST, 2 * W - D), BF)], axis=1)
    out_ref[:, D:] = tn(pick, jnp.concatenate([low, high], axis=0)).astype(BF)


def head_window(head):
    first = head * E // 128 * 128
    last = -(-(head + 1) * E // 128) * 128
    lane = iota((1, last - first), 1) + first
    keep = one_hot((lane >= head * E) & (lane < (head + 1) * E))
    return slice(first, last), keep


def frame_marks(mask_ref, rank):
    row = mask_ref[pl.ds(rank, 1), :].astype(F32)
    return jnp.transpose(jnp.broadcast_to(row, (128, N)))


def patch_marks(mask_ref, rank):
    shape = (N, F)
    spread = nn(one_hot((iota(shape, 0) & 31) == iota(shape, 1)), mask_ref[...].astype(F32).astype(BF))
    place = iota((N, N), 0) >> 5
    patch = jnp.where(place < 8, rank * 8 + place, LATE + rank * 4 + place - 8)
    chosen = jnp.where(patch == iota((N, N), 1), spread, 0.0)
    return jnp.broadcast_to(jnp.sum(chosen, axis=1, keepdims=True), (N, 128))


def modulation(mod_ref, step, row, marks, rows):
    clean = mod_ref[0, row : row + 1, :]
    noised = mod_ref[step, row : row + 1, :]
    wide = jnp.concatenate([marks[rows]] * (D // 128), axis=1)
    return jnp.where(wide == 1.0, clean, noised)


def chunks(size):
    return [slice(i, i + size) for i in range(0, N, size)]


def normalize(x):
    centered = x - jnp.mean(x, axis=1, keepdims=True)
    inverse = lax.rsqrt(jnp.mean(centered * centered, axis=1, keepdims=True) + 1e-06)
    return centered * inverse, inverse


def project(normed, w_ref, q_ref, k_ref, v_ref):
    inside = iota((1, W), 1) < HD
    q_ref[...] = jnp.where(inside, nn(normed, w_ref[:, :W]), 0.0).astype(BF)
    k = pltpu.roll(nn(normed, w_ref[:, 2 * HD - W : 2 * HD]), HD, 1)
    k_ref[...] = jnp.where(inside, k, 0.0).astype(BF)
    v_ref[:, :HD] = nn(normed, w_ref[:, 2 * HD :]).astype(BF)
    v_ref[:, HD:] = jnp.zeros((N, W - HD), BF)


def attend(q_ref, k_ref, v_ref, probs_ref, heads_acc, groups, same=None):
    heads_acc[...] = jnp.zeros((N, W), F32)
    for rows in groups:
        for head in range(H):
            lanes, keep = head_window(head)
            scores = nt(k_ref[rows, lanes], q_ref[rows, lanes] * keep)
            if same is not None:
                scores = jnp.where(same, scores, -1e30)
            top = jnp.max(scores, axis=0, keepdims=True)
            expo = jnp.exp2((scores - top) * (SCALE * math.log2(math.e)))
            probs = (expo * (1.0 / jnp.sum(expo, axis=0, keepdims=True))).astype(BF)
            probs_ref[head, rows, :] = probs
            heads_acc[rows, lanes] += tn(probs, v_ref[rows, lanes] * keep)


def attend_back(q_ref, k_ref, v_ref, probs_ref, dheads_ref, dq, dk, dv, groups):
    for acc in (dq, dk, dv):
        acc[...] = jnp.zeros((N, W), F32)
    for rows in groups:
        for head in range(H):
            lanes, keep = head_window(head)
            dhead = dheads_ref[rows, lanes] * keep
            probs = probs_ref[head, rows, :]
            wide = probs.astype(F32)
            dprobs = nt(v_ref[rows, lanes], dhead)
            total = jnp.sum(wide * dprobs, axis=0, keepdims=True)
            dscores = (wide * (dprobs - total)).astype(BF)
            dv[rows, lanes] += nn(probs, dhead)
            dk[rows, lanes] += nn(dscores, q_ref[rows, lanes] * keep)
            dq[rows, lanes] += tn(dscores, k_ref[rows, lanes] * keep)


def gather_dqkv(dq, dk, dv, dqkv_ref):
    low = pltpu.roll(dk[...] * SCALE, W - HD, 1)
    query = dq[...] * SCALE
    dqkv_ref[:, : W - 128] = query[:, : W - 128].astype(BF)
    dqkv_ref[:, W - 128 : W] = (query[:, W - 128 :] + low[:, :128]).astype(BF)
    dqkv_ref[:, W : 2 * HD] = low[:, 128:].astype(BF)
    dqkv_ref[:, 2 * HD :] = dv[...].astype(BF)


def split_halves(core, array_ref, half, keep_ref, send_ref):
    @pl.when(core == 0)
    def _():
        keep_ref[...] = array_ref[:, :half]
        send_ref[...] = array_ref[:, half:]

    @pl.when(core == 1)
    def _():
        keep_ref[...] = array_ref[:, half:]
        send_ref[...] = array_ref[:, :half]


def gated(dout_ref, mod_ref, step, row, marks, dattn_ref):
    for rows in chunks(128):
        gate = modulation(mod_ref, step, row, marks, rows)
        dattn_ref[rows, :D] = (dout_ref[rows, :].astype(F32) * gate).astype(BF)
    dattn_ref[:, D:] = jnp.zeros((N, 2 * GO - D), BF)


def input_gradient(x_ref, dout_ref, dnormed_ref, mod_ref, step, row, marks, out_ref):
    for rows in chunks(128):
        xhat, inverse = normalize(x_ref[rows, :].astype(F32))
        scale = 1.0 + modulation(mod_ref, step, row, marks, rows)
        dxhat = dnormed_ref[rows, :] * scale
        first = jnp.mean(dxhat, axis=1, keepdims=True)
        second = jnp.mean(dxhat * xhat, axis=1, keepdims=True)
        line = inverse * (dxhat - first - xhat * second)
        out_ref[rows, :] = (dout_ref[rows, :].astype(F32) + line).astype(out_ref.dtype)


def norm_rows(x_ref, mod_ref, step, row, marks, normed_ref):
    for rows in chunks(128):
        xhat, _ = normalize(x_ref[rows, :].astype(F32))
        shift = modulation(mod_ref, step, row, marks, rows)
        scale = modulation(mod_ref, step, row + 1, marks, rows)
        normed_ref[rows, :] = (xhat * (1.0 + scale) + shift).astype(BF)


def pack_cotangent(s_ref, cot_ref, out_ref):
    pack_frame(cot_ref[...], out_ref)


def spatial_forward(
    s_ref, x_ref, mask_ref, mod_ref, wqkv_ref, wo_ref,
    packed_ref, normed_ref, q_ref, k_ref, v_ref, probs_ref, heads_ref, acc, mid,
):
    marks = frame_marks(mask_ref, s_ref[0])
    step = s_ref[2]
    norm_rows(x_ref, mod_ref, step, 0, marks, normed_ref)
    project(normed_ref[...], wqkv_ref, q_ref, k_ref, v_ref)
    attend(q_ref, k_ref, v_ref, probs_ref, acc, [slice(0, N)])
    heads_ref[...] = acc[...].astype(BF)
    attn = nn(heads_ref[:, :HD], wo_ref[...])
    for rows in chunks(128):
        gate = modulation(mod_ref, step, 2, marks, rows)
        mid[rows, :] = (x_ref[rows, :].astype(F32) + gate * attn[rows]).astype(BF)
    pack_frame(mid[...], packed_ref)


def temporal(
    s_ref, mid_ref, cot_ref, mask_ref, mod_ref, wqkv_ref, wo_ref,
    packed_ref, normed_ref, heads_ref, qkeep_ref, qsend_ref, okeep_ref, osend_ref,
    x, dout, q, k, v, probs, acc, dq, dk, dv, dqkv, dattn, dheads, dnormed, dmid,
):
    step = s_ref[2]
    marks = patch_marks(mask_ref, s_ref[0])
    pick = patch_pick()
    x[...] = unpack_patches(mid_ref, pick)
    dout[...] = unpack_patches(cot_ref, pick)
    norm_rows(x, mod_ref, step, 3, marks, normed_ref)
    project(normed_ref[...], wqkv_ref, q, k, v)
    groups = chunks(128)
    same = (iota((128, 128), 0) >> 5) == (iota((128, 128), 1) >> 5)
    attend(q, k, v, probs, acc, groups, same)
    heads_ref[...] = acc[...].astype(BF)
    gated(dout, mod_ref, step, 5, marks, dattn)
    dheads[:, :HD] = nt(dattn[:, :D], wo_ref[...]).astype(BF)
    dheads[:, HD:] = jnp.zeros((N, W - HD), BF)
    attend_back(q, k, v, probs, dheads, dq, dk, dv, groups)
    gather_dqkv(dq, dk, dv, dqkv)
    dnormed[...] = nt(dqkv[:, : 3 * HD], wqkv_ref[...])
    input_gradient(x, dout, dnormed, mod_ref, step, 4, marks, dmid)
    pack_patches(dmid[...], pick, packed_ref)
    split_halves(s_ref[1], dqkv, GQ, qkeep_ref, qsend_ref)
    split_halves(s_ref[1], dattn, GO, okeep_ref, osend_ref)


def spatial_heads(s_ref, got_ref, mask_ref, mod_ref, wo_ref, dmid_ref, dheads_ref, keep_ref, send_ref, dattn):
    marks = frame_marks(mask_ref, s_ref[0])
    first, rest = unpack_frame(got_ref)
    dmid_ref[:LATE, :] = first
    dmid_ref[LATE:, :] = rest
    gated(dmid_ref, mod_ref, s_ref[2], 2, marks, dattn)
    dheads_ref[:, :HD] = nt(dattn[:, :D], wo_ref[...]).astype(BF)
    dheads_ref[:, HD:] = jnp.zeros((N, W - HD), BF)
    split_halves(s_ref[1], dattn, GO, keep_ref, send_ref)


def spatial_attention_back(
    s_ref, q_ref, k_ref, v_ref, probs_ref, dheads_ref,
    dqkv_ref, keep_ref, send_ref, dq, dk, dv,
):
    attend_back(q_ref, k_ref, v_ref, probs_ref, dheads_ref, dq, dk, dv, [slice(0, N)])
    gather_dqkv(dq, dk, dv, dqkv_ref)
    split_halves(s_ref[1], dqkv_ref, GQ, keep_ref, send_ref)


def spatial_input(s_ref, dqkv_ref, dmid_ref, x_ref, mask_ref, mod_ref, wqkv_ref, out_ref, dnormed):
    marks = frame_marks(mask_ref, s_ref[0])
    dnormed[...] = nt(dqkv_ref[:, : 3 * HD], wqkv_ref[...])
    input_gradient(x_ref, dmid_ref, dnormed, mod_ref, s_ref[2], 1, marks, out_ref)


def turn(s_ref, normed_ref, heads_ref, out_ref, wide, tall):
    wide[:D, :] = jnp.transpose(normed_ref[...].astype(F32))
    wide[D:, :] = jnp.zeros((8, N), F32)
    tall[:W, :] = jnp.transpose(heads_ref[...].astype(F32))
    tall[W:, :] = jnp.zeros((8, N), F32)
    place = iota((8, N), 0)
    for i in range(0, F, 2):
        fours, twos = [], []
        for j in (i, i + 1):
            out_ref[32 * j : 32 * j + 32, :] = wide[36 * j : 36 * j + 32, :].astype(BF)
            out_ref[1280 + 16 * j : 1296 + 16 * j, :] = tall[18 * j : 18 * j + 16, :].astype(BF)
            base = 36 * j + 32
            fours.append(jnp.where(place < 4, wide[base : base + 8, :], wide[base - 4 : base + 4, :]))
            base = 18 * j + 16
            two = tall[base : base + 8, :]
            for shift in (2, 4, 6):
                two = jnp.where(place < shift, two, tall[base - shift : base - shift + 8, :])
            twos.append(two)
        out_ref[1024 + 8 * i : 1040 + 8 * i, :] = jnp.concatenate(fours, axis=0).astype(BF)
        out_ref[1792 + 8 * i : 1808 + 8 * i, :] = jnp.concatenate(twos, axis=0).astype(BF)


def weight_shares(s_ref, a_ref, b_ref, qkeep_ref, qgot_ref, okeep_ref, ogot_ref, out_ref):
    def both(rows):
        return jnp.concatenate([a_ref[rows, :], b_ref[rows, :]], axis=1)

    def pair(one, two, lanes):
        return jnp.concatenate([one[:, lanes], two[:, lanes]], axis=0)

    main, rest = both(slice(0, 1024)), both(slice(1024, 1280))
    place = iota((F * 8, 128), 0) & 7
    extra = []
    for j in range(0, 7, 2):
        lanes = slice(128 * j, min(128 * j + 256, GQ))
        right = pair(qkeep_ref, qgot_ref, lanes)
        part = nn(main, right).astype(BF)
        out_ref[:, 32 * j : 32 * j + 32, :] = part[:, :128].reshape(F, 32, 128)
        last = nn(rest, right)
        if j < 6:
            out_ref[:, 32 * j + 32 : 32 * j + 64, :] = part[:, 128:].reshape(F, 32, 128)
            last = jnp.where(place < 4, last[:, :128], last[:, 128:])
        extra.append(last.reshape(F, 8, 128))
    main, rest = both(slice(1280, 1792)), both(slice(1792, 2048))
    right = pair(okeep_ref, ogot_ref, slice(0, GO))
    part, last = nn(main, right).astype(BF), nn(rest, right)
    for j in range(5):
        out_ref[:, 224 + 16 * j : 240 + 16 * j, :] = part[:, 128 * j : 128 * j + 128].reshape(F, 16, 128)
    four = last[:, :128]
    for j in (1, 2, 3):
        four = jnp.where(place < 2 * j, four, last[:, 128 * j : 128 * j + 128])
    extra += [four.reshape(F, 8, 128), last[:, 512:].reshape(F, 8, 128)]
    for j in range(3):
        both_extra = jnp.concatenate(extra[2 * j : 2 * j + 2], axis=1)
        out_ref[:, 304 + 16 * j : 320 + 16 * j, :] = both_extra.astype(BF)


def sum_shares(s_ref, got_ref, out_ref):
    for start in range(0, ROWS, 32):
        total = got_ref[0, start : start + 32, :].astype(F32)
        for i in range(1, F):
            total = total + got_ref[i, start : start + 32, :].astype(F32)
        out_ref[start : start + 32, :] = total


def finish(s_ref, own_ref, one_ref, two_ref, three_ref, gq_ref, go_ref):
    factor = 1.0 / math.sqrt(4 * F * N)
    same = (own_ref[...] + two_ref[...]) * factor
    other = (one_ref[...] + three_ref[...]) * factor
    core = s_ref[1]
    halves = [jnp.where(core == 0, same, other), jnp.where(core == 0, other, same)]
    for side, half in enumerate(halves):
        for j in range(7):
            start = GQ * side + 128 * j
            width = min(128, 3 * HD - start)
            gq_ref[:32, start : start + width] = half[32 * j : 32 * j + 32, :width]
            base = 304 + 4 * j
            gq_ref[32:, start : start + width] = half[base : base + 4, :width]
        for j in range(5):
            start = GO * side + 128 * j
            if start < D:
                go_ref[:16, start : start + 128] = half[224 + 16 * j : 240 + 16 * j, :]
                go_ref[16:, start : start + 128] = half[336 + 2 * j : 338 + 2 * j, :]


def over_cores(array):
    return lax.ppermute(array, "dp", [(0, 1), (1, 0), (2, 3), (3, 2)])


def exchange(packed):
    shape = packed.shape
    sent = lax.all_to_all(packed.reshape(F, shape[0] // F, shape[1]), "seq", 0, 0, tiled=True)
    return sent.reshape(shape)


def reduce_weights(scalars, turned, turned_other, qkeep, qgot, okeep, ogot):
    shares = call(
        weight_shares, [((F, ROWS, 128), BF)], scalars, turned, turned_other, qkeep, qgot, okeep, ogot
    )[0]
    got = lax.all_to_all(shares, "seq", 0, 0, tiled=True)
    own = call(sum_shares, [((ROWS, 128), F32)], scalars, got)[0]
    others = [lax.ppermute(own, "dp", [(i, (i + k) % 4) for i in range(4)]) for k in (1, 2, 3)]
    return call(finish, [((36, 3 * HD), F32), ((18, D), F32)], scalars, own, *others)


def body(tokens, cotangent, mask, t_index, mod_table, wqkv_s, wo_s, wqkv_t, wo_t):
    scalars = jnp.stack([lax.axis_index("seq"), lax.axis_index("dp") & 1, t_index[0]]).astype(jnp.int32)
    x, cot, marks = tokens[0, 0], cotangent[0, 0], mask[0]
    cot = exchange(call(pack_cotangent, [((LATE, PACK), BF)], scalars, cot)[0])
    packed, normed_s, q, k, v, probs, heads_s = call(
        spatial_forward,
        [((LATE, PACK), BF), ((N, D), BF)] + [((N, W), BF)] * 3 + [((H, N, N), BF), ((N, W), BF)],
        scalars, x, marks, mod_table, wqkv_s, wo_s,
        scratch=[((N, W), F32), ((N, D), BF)],
    )
    mid = exchange(packed)
    turn_scratch = [((D + 8, N), F32), ((W + 8, N), F32)]
    turned_s = call(turn, [((2048, N), BF)], scalars, normed_s, heads_s, scratch=turn_scratch)[0]
    other_s = over_cores(turned_s)
    halves_q, halves_o = [((N, GQ), BF)] * 2, [((N, GO), BF)] * 2
    packed, normed_t, heads_t, qkeep, qsend, okeep, osend = call(
        temporal,
        [((LATE, PACK), BF), ((N, D), BF), ((N, W), BF)] + halves_q + halves_o,
        scalars, mid, cot, marks, mod_table, wqkv_t, wo_t,
        scratch=[((N, D), BF)] * 2 + [((N, W), BF)] * 3 + [((H, N, 128), BF)] + [((N, W), F32)] * 4
        + [((N, PACK), BF), ((N, 2 * GO), BF), ((N, W), BF), ((N, D), F32), ((N, D), BF)],
    )
    got = exchange(packed)
    turned_t = call(turn, [((2048, N), BF)], scalars, normed_t, heads_t, scratch=turn_scratch)[0]
    grads_t = reduce_weights(
        scalars, turned_t, over_cores(turned_t), qkeep, over_cores(qsend), okeep, over_cores(osend)
    )
    dmid, dheads, okeep, osend = call(
        spatial_heads,
        [((N, D), BF), ((N, W), BF)] + halves_o,
        scalars, got, marks, mod_table, wo_s,
        scratch=[((N, 2 * GO), BF)],
    )
    dqkv, qkeep, qsend = call(
        spatial_attention_back,
        [((N, PACK), BF)] + halves_q,
        scalars, q, k, v, probs, dheads,
        scratch=[((N, W), F32)] * 3,
    )
    grads_s = reduce_weights(
        scalars, turned_s, other_s, qkeep, over_cores(qsend), okeep, over_cores(osend)
    )
    grad = call(
        spatial_input, [((N, D), F32)], scalars, dqkv, dmid, x, marks, mod_table, wqkv_s,
        scratch=[((N, D), F32)],
    )[0]
    return (grad[None, None], *grads_s, *grads_t)


def solution(mesh):
    return jax.shard_map(
        body,
        mesh=mesh,
        in_specs=(
            P("dp", "seq", None, None),
            P("dp", "seq", None, None),
            P("dp", None, None),
            P("dp"),
            P(),
            P(),
            P(),
            P(),
            P(),
        ),
        out_specs=(
            P("dp", "seq", None, None),
            P("seq", None),
            P("seq", None),
            P("seq", None),
            P("seq", None),
        ),
        check_vma=False,
    )
```

```python
import math

import jax
import jax.numpy as jnp
from jax import lax
from jax.experimental import pallas as pl
from jax.experimental.pallas import tpu as pltpu
from jax.sharding import Mesh
from jax.sharding import PartitionSpec as P

D = 1152
H = 8
E = 72
HD = 576
N = 384
F = 32
W = 640
LATE = 256
REST = 128
PACK = 1792
GQ = 896
GO = 640
ROWS = 352
BF = jnp.bfloat16
F32 = jnp.float32
SCALE = E**-0.5
SEQ = ("x", "zh", "y")
SMEM = pl.BlockSpec(memory_space=pltpu.SMEM)
ANY = pl.BlockSpec(memory_space=pl.ANY)


class Moves:
    def __init__(self, sems):
        self.sems, self.used, self.coming, self.going = sems, 0, {}, {}

    def copy(self, source, target):
        made = pltpu.make_async_copy(source, target, self.sems.at[self.used])
        self.used += 1
        made.start()
        return made

    def need(self, ref, part=0):
        made = self.coming[id(ref)][part]
        if made is not None:
            made.wait()
            self.coming[id(ref)][part] = None

    def done(self, ref, index=None):
        target, sent = self.going[id(ref)]
        if index is None:
            sent.append(self.copy(ref, target))
        else:
            sent.append(self.copy(ref.at[index], target.at[index]))

    def close(self, ins, outs):
        for ref in ins:
            for part in range(len(self.coming[id(ref)])):
                self.need(ref, part)
        for ref in outs:
            if not self.going[id(ref)][1]:
                self.done(ref)
        for ref in outs:
            for made in self.going[id(ref)][1]:
                made.wait()


def call(kernel, out, *args, scratch=(), cost=None, parts=None, pieces=0):
    arrays = args[1:]
    count, last = len(arrays), len(arrays) + len(out)
    parts = parts or {}
    cuts = [parts.get(i, [None]) for i in range(count)]
    copies = sum(len(cut) for cut in cuts) + len(out) + pieces

    def whole(s_ref, *refs):
        far, near = refs[:last], refs[last : 2 * last]
        io = Moves(refs[-1])
        for ref, cut in zip(near[:count], cuts):
            io.coming[id(ref)] = [None] * len(cut)
        for step in range(max(len(cut) for cut in cuts)):
            for source, ref, cut in zip(far[:count], near[:count], cuts):
                if step < len(cut):
                    at = cut[step]
                    pair = (source, ref) if at is None else (source.at[at], ref.at[at])
                    io.coming[id(ref)][step] = io.copy(*pair)
        for target, ref in zip(far[count:], near[count:]):
            io.going[id(ref)] = (target, [])
        kernel(io, s_ref, *near, *refs[2 * last : -1])
        io.close(near[:count], near[count:])

    near = [pltpu.VMEM(array.shape, array.dtype) for array in arrays]
    near += [pltpu.VMEM(shape, kind) for shape, kind in out]
    return pl.pallas_call(
        whole,
        out_shape=[jax.ShapeDtypeStruct(shape, kind) for shape, kind in out],
        in_specs=[SMEM] + [ANY] * count,
        out_specs=[ANY] * len(out),
        scratch_shapes=near
        + [pltpu.VMEM(shape, kind) for shape, kind in scratch]
        + [pltpu.SemaphoreType.DMA((copies,))],
        compiler_params=pltpu.CompilerParams(vmem_limit_bytes=56 * 1024 * 1024),
        cost_estimate=cost,
        name=kernel.__name__,
    )(*args)


LIGHT = pl.CostEstimate(flops=1000, transcendentals=0, bytes_accessed=1000)


def nn(a, b):
    return lax.dot_general(a, b, (((1,), (0,)), ((), ())), preferred_element_type=F32)


def nt(a, b):
    return lax.dot_general(a, b, (((1,), (1,)), ((), ())), preferred_element_type=F32)


def tn(a, b):
    return lax.dot_general(a, b, (((0,), (0,)), ((), ())), preferred_element_type=F32)


def iota(shape, dim):
    return lax.broadcasted_iota(jnp.int32, shape, dim)


def one_hot(test):
    return jnp.where(test, 1.0, 0.0).astype(BF)


def rest_pick(back):
    shape = (LATE, 2 * REST)
    row, col = iota(shape, 0), iota(shape, 1)
    if back:
        shape = (2 * REST, LATE)
        row, col = iota(shape, 1), iota(shape, 0)
    return one_hot((row & 3) + 4 * (row >> 3) + REST * ((row >> 2) & 1) == col)


def pack_frame(rows, out_ref, at):
    out_ref[:, at : at + D] = rows[:LATE]
    low = rows[LATE:, :W]
    high = jnp.concatenate([rows[LATE:, W:], jnp.zeros((REST, 2 * W - D), BF)], axis=1)
    both = jnp.concatenate([low, high], axis=0)
    out_ref[:, at + D : at + PACK] = nn(rest_pick(False), both).astype(BF)


def unpack_frame(got_ref):
    both = nn(rest_pick(True), got_ref[:, D:])
    rest = jnp.concatenate([both[:REST], both[REST:, : D - W]], axis=1).astype(BF)
    return got_ref[:, :D], rest


def patch_pick():
    shape = (LATE, LATE)
    row, col = iota(shape, 0), iota(shape, 1)
    return one_hot((row & 31) * 8 + (row >> 5) == col)


def unpack_patches(got_ref, pick, at):
    first = nn(pick, got_ref[:, at : at + D])
    rest = nn(pick, got_ref[:, at + D : at + PACK])
    rest = jnp.concatenate([rest[:REST], rest[REST:, : D - W]], axis=1)
    return jnp.concatenate([first, rest], axis=0).astype(BF)


def pack_patches(rows, pick, out_ref):
    out_ref[:, :D] = tn(pick, rows[:LATE]).astype(BF)
    low = rows[LATE:, :W]
    high = jnp.concatenate([rows[LATE:, W:], jnp.zeros((REST, 2 * W - D), BF)], axis=1)
    out_ref[:, D:] = tn(pick, jnp.concatenate([low, high], axis=0)).astype(BF)


def head_window(head):
    first = head * E // 128 * 128
    last = -(-(head + 1) * E // 128) * 128
    lane = iota((1, last - first), 1) + first
    keep = one_hot((lane >= head * E) & (lane < (head + 1) * E))
    return slice(first, last), keep


def frame_marks(mask_ref, rank):
    row = mask_ref[pl.ds(rank, 1), :].astype(F32)
    return jnp.transpose(jnp.broadcast_to(row, (128, N)))


def patch_marks(mask_ref, rank):
    shape = (N, F)
    spread = nn(one_hot((iota(shape, 0) & 31) == iota(shape, 1)), mask_ref[...].astype(F32).astype(BF))
    place = iota((N, N), 0) >> 5
    patch = jnp.where(place < 8, rank * 8 + place, LATE + rank * 4 + place - 8)
    chosen = jnp.where(patch == iota((N, N), 1), spread, 0.0)
    return jnp.broadcast_to(jnp.sum(chosen, axis=1, keepdims=True), (N, 128))


def modulation(mod_ref, step, row, marks, rows):
    clean = mod_ref[row, 0:1, :]
    noised = mod_ref[row, pl.ds(step, 1), :]
    wide = jnp.concatenate([marks[rows]] * (D // 128), axis=1)
    return jnp.where(wide == 1.0, clean, noised)


def chunks(size):
    return [slice(i, i + size) for i in range(0, N, size)]


def normalize(x):
    centered = x - jnp.mean(x, axis=1, keepdims=True)
    inverse = lax.rsqrt(jnp.mean(centered * centered, axis=1, keepdims=True) + 1e-06)
    return centered * inverse, inverse


def project(normed, w_ref, q_ref, k_ref, v_ref):
    for i, ref in enumerate((q_ref, k_ref, v_ref)):
        ref[:, :HD] = nt(normed, w_ref[HD * i : HD * i + HD, :]).astype(BF)
        ref[:, HD:] = jnp.zeros((N, W - HD), BF)


class Blocks:
    def __init__(self):
        self.parts = [[] for _ in range(W // 128)]

    def add(self, lanes, value):
        for i in range((lanes.stop - lanes.start) // 128):
            self.parts[lanes.start // 128 + i].append(value[:, 128 * i : 128 * i + 128])

    def join(self):
        return jnp.concatenate([sum(parts[1:], parts[0]) for parts in self.parts], axis=1)


def attend(q_ref, k_ref, v_ref, probs_ref, heads_ref, groups, same=None):
    for rows in groups:
        heads = Blocks()
        for head in range(H):
            lanes, keep = head_window(head)
            scores = nt(k_ref[rows, lanes], q_ref[rows, lanes] * keep)
            if same is not None:
                scores = jnp.where(same, scores, -1e30)
            top = jnp.max(scores, axis=0, keepdims=True)
            expo = jnp.exp2((scores - top) * (SCALE * math.log2(math.e)))
            probs = (expo * (1.0 / jnp.sum(expo, axis=0, keepdims=True))).astype(BF)
            probs_ref[head, rows, :] = probs
            heads.add(lanes, tn(probs, v_ref[rows, lanes] * keep))
        heads_ref[rows, :] = heads.join().astype(BF)


def attend_back(q_ref, k_ref, v_ref, probs_ref, dheads_ref, dqkv_ref, groups):
    for rows in groups:
        dq, dk, dv = Blocks(), Blocks(), Blocks()
        for head in range(H):
            lanes, keep = head_window(head)
            dhead = dheads_ref[rows, lanes] * keep
            probs = probs_ref[head, rows, :]
            wide = probs.astype(F32)
            dprobs = nt(v_ref[rows, lanes], dhead)
            total = jnp.sum(wide * dprobs, axis=0, keepdims=True)
            dscores = (wide * (dprobs - total)).astype(BF)
            dv.add(lanes, nn(probs, dhead))
            dk.add(lanes, nn(dscores, q_ref[rows, lanes] * keep))
            dq.add(lanes, tn(dscores, k_ref[rows, lanes] * keep))
        query, low = dq.join() * SCALE, pltpu.roll(dk.join() * SCALE, W - HD, 1)
        dqkv_ref[rows, : W - 128] = query[:, : W - 128].astype(BF)
        dqkv_ref[rows, W - 128 : W] = (query[:, W - 128 :] + low[:, :128]).astype(BF)
        dqkv_ref[rows, W : 2 * HD] = low[:, 128:].astype(BF)
        dqkv_ref[rows, 2 * HD :] = dv.join().astype(BF)


def split_halves(core, dqkv_ref, dattn_ref, keep_ref, send_ref):
    def take(ref, side):
        ref[:, :GQ] = dqkv_ref[:, GQ * side : GQ * side + GQ]
        ref[:, GQ:] = dattn_ref[:, GO * side : GO * side + GO]

    @pl.when(core == 0)
    def _():
        take(keep_ref, 0)
        take(send_ref, 1)

    @pl.when(core == 1)
    def _():
        take(keep_ref, 1)
        take(send_ref, 0)


def gated(dout_ref, mod_ref, step, row, marks, dattn_ref):
    for rows in chunks(128):
        gate = modulation(mod_ref, step, row, marks, rows)
        dattn_ref[rows, :D] = (dout_ref[rows, :].astype(F32) * gate).astype(BF)
    dattn_ref[:, D:] = jnp.zeros((N, 2 * GO - D), BF)


def input_gradient(x_ref, dout_ref, dnormed_ref, mod_ref, step, row, marks, out_ref):
    for rows in chunks(128):
        xhat, inverse = normalize(x_ref[rows, :].astype(F32))
        scale = 1.0 + modulation(mod_ref, step, row, marks, rows)
        dxhat = dnormed_ref[rows, :] * scale
        first = jnp.mean(dxhat, axis=1, keepdims=True)
        second = jnp.mean(dxhat * xhat, axis=1, keepdims=True)
        line = inverse * (dxhat - first - xhat * second)
        out_ref[rows, :] = (dout_ref[rows, :].astype(F32) + line).astype(out_ref.dtype)


def norm_rows(x_ref, mod_ref, step, row, marks, normed_ref):
    for rows in chunks(128):
        xhat, _ = normalize(x_ref[rows, :].astype(F32))
        shift = modulation(mod_ref, step, row, marks, rows)
        scale = modulation(mod_ref, step, row + 1, marks, rows)
        normed_ref[rows, :] = (xhat * (1.0 + scale) + shift).astype(BF)


def spatial_forward(
    io, s_ref, x_ref, mask_ref, mod_ref, wqkv_ref, wo_ref, cot_ref,
    packed_ref, normed_ref, q_ref, k_ref, v_ref, probs_ref, heads_ref, mid,
):
    step = s_ref[2]
    io.need(mask_ref)
    marks = frame_marks(mask_ref, s_ref[0])
    io.need(x_ref)
    io.need(mod_ref)
    norm_rows(x_ref, mod_ref, step, 0, marks, normed_ref)
    io.done(normed_ref)
    io.need(wqkv_ref)
    project(normed_ref[...], wqkv_ref, q_ref, k_ref, v_ref)
    for ref in (q_ref, k_ref, v_ref):
        io.done(ref)
    attend(q_ref, k_ref, v_ref, probs_ref, heads_ref, [slice(0, N)])
    io.done(probs_ref)
    io.done(heads_ref)
    io.need(cot_ref)
    pack_frame(cot_ref[...], packed_ref, PACK)
    io.need(wo_ref)
    attn = nn(heads_ref[:, :HD], wo_ref[...])
    for rows in chunks(128):
        gate = modulation(mod_ref, step, 2, marks, rows)
        mid[rows, :] = (x_ref[rows, :].astype(F32) + gate * attn[rows]).astype(BF)
    pack_frame(mid[...], packed_ref, 0)


def temporal(
    io, s_ref, got_ref, mask_ref, mod_ref, wqkv_ref, wo_ref,
    packed_ref, normed_ref, heads_ref, keep_ref, send_ref,
    x, dout, q, k, v, probs, dqkv, dattn, dheads, dnormed, dmid,
):
    step = s_ref[2]
    io.need(mask_ref)
    marks = patch_marks(mask_ref, s_ref[0])
    pick = patch_pick()
    io.need(got_ref)
    x[...] = unpack_patches(got_ref, pick, 0)
    io.need(mod_ref)
    norm_rows(x, mod_ref, step, 3, marks, normed_ref)
    io.done(normed_ref)
    io.need(wqkv_ref)
    project(normed_ref[...], wqkv_ref, q, k, v)
    groups = chunks(128)
    same = (iota((128, 128), 0) >> 5) == (iota((128, 128), 1) >> 5)
    attend(q, k, v, probs, heads_ref, groups, same)
    io.done(heads_ref)
    dout[...] = unpack_patches(got_ref, pick, PACK)
    gated(dout, mod_ref, step, 5, marks, dattn)
    io.need(wo_ref)
    dheads[:, :HD] = nt(dattn[:, :D], wo_ref[...]).astype(BF)
    dheads[:, HD:] = jnp.zeros((N, W - HD), BF)
    attend_back(q, k, v, probs, dheads, dqkv, groups)
    split_halves(s_ref[1], dqkv, dattn, keep_ref, send_ref)
    io.done(send_ref)
    io.done(keep_ref)
    dnormed[...] = nn(dqkv[:, : 3 * HD], wqkv_ref[...])
    input_gradient(x, dout, dnormed, mod_ref, step, 4, marks, dmid)
    pack_patches(dmid[...], pick, packed_ref)


def spatial_back(
    io, s_ref, got_ref, mask_ref, mod_ref, wo_ref, v_ref, probs_ref, q_ref, k_ref,
    dmid_ref, dqkv_ref, keep_ref, send_ref, dattn, dheads,
):
    io.need(mask_ref)
    marks = frame_marks(mask_ref, s_ref[0])
    io.need(got_ref)
    first, rest = unpack_frame(got_ref)
    dmid_ref[:LATE, :] = first
    dmid_ref[LATE:, :] = rest
    io.done(dmid_ref)
    io.need(mod_ref)
    gated(dmid_ref, mod_ref, s_ref[2], 2, marks, dattn)
    io.need(wo_ref)
    dheads[:, :HD] = nt(dattn[:, :D], wo_ref[...]).astype(BF)
    dheads[:, HD:] = jnp.zeros((N, W - HD), BF)
    for ref in (v_ref, probs_ref, q_ref, k_ref):
        io.need(ref)
    attend_back(q_ref, k_ref, v_ref, probs_ref, dheads, dqkv_ref, [slice(0, N)])
    io.done(dqkv_ref)
    split_halves(s_ref[1], dqkv_ref, dattn, keep_ref, send_ref)


def spatial_input(io, s_ref, dqkv_ref, wqkv_ref, dmid_ref, x_ref, mask_ref, mod_ref, out_ref, dnormed):
    io.need(dqkv_ref)
    io.need(wqkv_ref)
    dnormed[...] = nn(dqkv_ref[:, : 3 * HD], wqkv_ref[...])
    for ref in (dmid_ref, x_ref, mask_ref, mod_ref):
        io.need(ref)
    marks = frame_marks(mask_ref, s_ref[0])
    input_gradient(x_ref, dmid_ref, dnormed, mod_ref, s_ref[2], 1, marks, out_ref)


def turn(normed_ref, heads_ref, out_ref, wide, tall, order):
    wide[:D, :] = jnp.transpose(normed_ref[...].astype(F32))
    wide[D:, :] = jnp.zeros((8, N), F32)
    tall[:W, :] = jnp.transpose(heads_ref[...].astype(F32))
    tall[W:, :] = jnp.zeros((8, N), F32)
    place = iota((8, N), 0)
    for i in range(0, F, 2):
        fours, twos = [], []
        for i_at, j in ((i, order[i]), (i + 1, order[i + 1])):
            out_ref[32 * i_at : 32 * i_at + 32, :] = wide[36 * j : 36 * j + 32, :].astype(BF)
            base = 1280 + 16 * i_at
            out_ref[base : base + 16, :] = tall[18 * j : 18 * j + 16, :].astype(BF)
            base = 36 * j + 32
            fours.append(jnp.where(place < 4, wide[base : base + 8, :], wide[base - 4 : base + 4, :]))
            base = 18 * j + 16
            two = tall[base : base + 8, :]
            for shift in (2, 4, 6):
                two = jnp.where(place < shift, two, tall[base - shift : base - shift + 8, :])
            twos.append(two)
        out_ref[1024 + 8 * i : 1040 + 8 * i, :] = jnp.concatenate(fours, axis=0).astype(BF)
        out_ref[1792 + 8 * i : 1808 + 8 * i, :] = jnp.concatenate(twos, axis=0).astype(BF)


def turn_spatial(io, s_ref, normed_ref, heads_ref, out_ref, wide, tall):
    io.need(normed_ref)
    io.need(heads_ref)
    turn(normed_ref, heads_ref, out_ref, wide, tall, range(F))


def turn_temporal(
    io, s_ref, normed_ref, heads_ref, normed_other_ref, heads_other_ref, own_ref, other_ref, wide, tall
):
    order = [i // 8 * 8 + i % 2 * 4 + i // 2 % 4 for i in range(F)]
    io.need(normed_ref)
    io.need(heads_ref)
    turn(normed_ref, heads_ref, own_ref, wide, tall, order)
    io.done(own_ref)
    io.need(normed_other_ref)
    io.need(heads_other_ref)
    turn(normed_other_ref, heads_other_ref, other_ref, wide, tall, order)


SHARE_PARTS = {
    0: [(slice(1280, 2048), slice(None)), (slice(0, 1280), slice(None))],
    1: [(slice(1280, 2048), slice(None)), (slice(0, 1280), slice(None))],
    2: [(slice(None), slice(GQ, GQ + GO)), (slice(None), slice(0, GQ))],
    3: [(slice(None), slice(GQ, GQ + GO)), (slice(None), slice(0, GQ))],
}


def weight_shares(io, s_ref, a_ref, b_ref, keep_ref, got_ref, out_ref):
    def both(rows):
        return jnp.concatenate([a_ref[rows, :], b_ref[rows, :]], axis=1)

    def pair(lanes):
        return jnp.concatenate([keep_ref[:, lanes], got_ref[:, lanes]], axis=0)

    def send(start, size):
        io.done(out_ref, (slice(None), slice(start, start + size), slice(None)))

    place = iota((F * 8, 128), 0) & 7
    for ref in (a_ref, b_ref, keep_ref, got_ref):
        io.need(ref, 0)
    main, rest = both(slice(1280, 1792)), both(slice(1792, 2048))
    right = pair(slice(GQ, GQ + GO))
    part, last = nn(main, right).astype(BF), nn(rest, right)
    for j in range(5):
        out_ref[:, 224 + 16 * j : 240 + 16 * j, :] = part[:, 128 * j : 128 * j + 128].reshape(F, 16, 128)
    four = last[:, :128]
    for j in (1, 2, 3):
        four = jnp.where(place < 2 * j, four, last[:, 128 * j : 128 * j + 128])
    both_extra = [four.reshape(F, 8, 128), last[:, 512:].reshape(F, 8, 128)]
    out_ref[:, 336:352, :] = jnp.concatenate(both_extra, axis=1).astype(BF)
    for ref in (a_ref, b_ref, keep_ref, got_ref):
        io.need(ref, 1)
    main, rest = both(slice(0, 1024)), both(slice(1024, 1280))
    extra = []
    for j in range(0, 7, 2):
        lanes = slice(128 * j, min(128 * j + 256, GQ))
        right = pair(lanes)
        part = nn(main, right).astype(BF)
        out_ref[:, 32 * j : 32 * j + 32, :] = part[:, :128].reshape(F, 32, 128)
        last = nn(rest, right)
        if j < 6:
            out_ref[:, 32 * j + 32 : 32 * j + 64, :] = part[:, 128:].reshape(F, 32, 128)
            last = jnp.where(place < 4, last[:, :128], last[:, 128:])
            send(32 * j, 64)
        extra.append(last.reshape(F, 8, 128))
    for j in range(2):
        both_extra = jnp.concatenate(extra[2 * j : 2 * j + 2], axis=1)
        out_ref[:, 304 + 16 * j : 320 + 16 * j, :] = both_extra.astype(BF)
    send(192, 160)


SUM_PARTS = [(slice(None), slice(i, i + 176), slice(None)) for i in (0, 176)]


def sum_all(io, s_ref, got_ref, clip_ref, far_ref, out_ref):
    for part in range(2):
        io.need(got_ref, part)
        for start in range(176 * part, 176 * part + 176, 16):
            total = got_ref[0, start : start + 16, :].astype(F32)
            for i in range(1, F):
                total = total + got_ref[i, start : start + 16, :].astype(F32)
            out_ref[start : start + 16, :] = total.astype(BF)
    io.need(clip_ref)
    io.need(far_ref)
    own = clip_ref[(s_ref[0] >> 2) & 1]
    out_ref[ROWS:, :] = (own.astype(F32) + far_ref[...].astype(F32)).astype(BF)


def finish(io, s_ref, own_ref, one_ref, two_ref, three_ref, gq_ref, go_ref, tq_ref, to_ref):
    factor = 1.0 / math.sqrt(4 * F * N)
    for ref in (own_ref, one_ref, two_ref, three_ref):
        io.need(ref)
    core = s_ref[1]
    for rows, q_ref, o_ref in ((slice(0, ROWS), gq_ref, go_ref), (slice(ROWS, 2 * ROWS), tq_ref, to_ref)):
        own, one, two, three = (
            ref[rows, :].astype(F32) for ref in (own_ref, one_ref, two_ref, three_ref)
        )
        same, other = (own + two) * factor, (one + three) * factor
        halves = [jnp.where(core == 0, same, other), jnp.where(core == 0, other, same)]
        for side, half in enumerate(halves):
            for j in range(7):
                start = GQ * side + 128 * j
                width = min(128, 3 * HD - start)
                q_ref[:32, start : start + width] = half[32 * j : 32 * j + 32, :width]
                base = 304 + 4 * j
                q_ref[32:, start : start + width] = half[base : base + 4, :width]
            for j in range(5):
                start = GO * side + 128 * j
                if start < D:
                    o_ref[:16, start : start + 128] = half[224 + 16 * j : 240 + 16 * j, :]
                    o_ref[16:, start : start + 128] = half[336 + 2 * j : 338 + 2 * j, :]
        io.done(q_ref)
        io.done(o_ref)


def over_cores(array):
    return lax.ppermute(array, "dp", [(0, 1), (1, 0), (2, 3), (3, 2)])


def exchange(packed):
    shape = packed.shape
    sent = lax.all_to_all(packed.reshape(F, shape[0] // F, shape[1]), SEQ, 0, 0, tiled=True)
    return sent.reshape(shape)


def body(tokens, cotangent, mask, t_index, mod_table, wqkv_s, wo_s, wqkv_t, wo_t):
    scalars = jnp.stack([lax.axis_index(SEQ), lax.axis_index("dp") & 1, t_index[0]]).astype(jnp.int32)
    x, cot, marks = tokens[0, 0], cotangent[0, 0], mask[0]
    mods, wqkv_s, wqkv_t = jnp.transpose(mod_table, (1, 0, 2)), wqkv_s.T, wqkv_t.T
    packed, normed_s, q, k, v, probs, heads_s = call(
        spatial_forward,
        [((LATE, 2 * PACK), BF), ((N, D), BF)] + [((N, W), BF)] * 3 + [((H, N, N), BF), ((N, W), BF)],
        scalars, x, marks, mods, wqkv_s, wo_s, cot,
        scratch=[((N, D), BF)],
    )
    got = exchange(packed)
    turn_scratch = [((D + 8, N), F32), ((W + 8, N), F32)]
    turned = [((2048, N), BF)]
    turned_s = call(turn_spatial, turned, scalars, normed_s, heads_s, scratch=turn_scratch, cost=LIGHT)[0]
    other_s = over_cores(turned_s)
    got, turned_s = lax.optimization_barrier((got, turned_s))
    halves = [((N, GQ + GO), BF)] * 2
    packed, normed_t, heads_t, keep, send = call(
        temporal,
        [((LATE, PACK), BF), ((N, D), BF), ((N, W), BF)] + halves,
        scalars, got, marks, mods, wqkv_t, wo_t,
        scratch=[((N, D), BF)] * 2 + [((N, W), BF)] * 3 + [((H, N, 128), BF)]
        + [((N, PACK), BF), ((N, 2 * GO), BF), ((N, W), BF), ((N, D), F32), ((N, D), BF)],
    )
    got = exchange(packed)
    turned_t, other_t = call(
        turn_temporal, turned * 2,
        scalars, normed_t, heads_t, over_cores(normed_t), over_cores(heads_t),
        scratch=turn_scratch, cost=LIGHT,
    )
    shares = [((F, ROWS, 128), BF)]
    shares_t = call(
        weight_shares, shares, scalars, turned_t, other_t, keep, over_cores(send),
        cost=LIGHT, parts=SHARE_PARTS, pieces=4,
    )[0]
    got, shares_t = lax.optimization_barrier((got, shares_t))
    shares_t = lax.psum_scatter(shares_t, "x", scatter_dimension=0, tiled=True)
    dmid, dqkv, keep, send = call(
        spatial_back,
        [((N, D), BF), ((N, PACK), BF)] + halves,
        scalars, got, marks, mods, wo_s, v, probs, q, k,
        scratch=[((N, 2 * GO), BF), ((N, W), BF)],
    )
    shares_s = call(
        weight_shares, shares, scalars, turned_s, other_s, keep, over_cores(send),
        parts=SHARE_PARTS, pieces=4,
    )[0]
    shares_s = lax.all_to_all(shares_s, SEQ, 0, 0, tiled=True)
    grad = call(
        spatial_input, [((N, D), F32)], scalars, dqkv, wqkv_s, dmid, x, marks, mods,
        scratch=[((N, D), F32)], cost=LIGHT,
    )[0]
    shares_t, grad = lax.optimization_barrier((shares_t, grad))
    shares_t = lax.psum_scatter(shares_t, "y", scatter_dimension=0, tiled=True)
    shares_s, grad = lax.optimization_barrier((shares_s, grad))
    send = lax.dynamic_index_in_dim(shares_t, 1 - lax.axis_index("zh"), 0, keepdims=False)
    far = lax.ppermute(send, "zh", [(0, 1), (1, 0)])
    own = call(
        sum_all, [((2 * ROWS, 128), BF)], scalars, shares_s, shares_t, far, parts={0: SUM_PARTS}
    )[0]
    others = [lax.ppermute(own, "dp", [(i, (i + k) % 4) for i in range(4)]) for k in (1, 2, 3)]
    results = call(finish, [((36, 3 * HD), F32), ((18, D), F32)] * 2, scalars, own, *others)
    return (grad[None, None], *results)


def solution(mesh):
    parts = Mesh(mesh.devices.reshape(4, 2, 4, 4), (*SEQ, "dp"))
    return jax.shard_map(
        body,
        mesh=parts,
        in_specs=(
            P("dp", SEQ, None, None),
            P("dp", SEQ, None, None),
            P("dp", None, None),
            P("dp"),
            P(),
            P(),
            P(),
            P(),
            P(),
        ),
        out_specs=(
            P("dp", SEQ, None, None),
            P(SEQ, None),
            P(SEQ, None),
            P(SEQ, None),
            P(SEQ, None),
        ),
        check_vma=False,
    )
```

```python
import math

import jax
import jax.numpy as jnp
from jax import lax
from jax.experimental import pallas as pl
from jax.experimental.pallas import tpu as pltpu
from jax.sharding import PartitionSpec as P

D = 1152
H = 8
E = 72
HD = 576
N = 384
F = 32
W = 640
LATE = 256
REST = 128
PACK = 1792
GQ = 896
GO = 640
ROWS = 352
BF = jnp.bfloat16
F32 = jnp.float32
SCALE = E**-0.5
SMEM = pl.BlockSpec(memory_space=pltpu.SMEM)
ANY = pl.BlockSpec(memory_space=pl.ANY)


class Moves:
    def __init__(self, sems):
        self.sems, self.used, self.coming, self.going = sems, 0, {}, {}

    def copy(self, source, target):
        made = pltpu.make_async_copy(source, target, self.sems.at[self.used])
        self.used += 1
        made.start()
        return made

    def need(self, ref, part=0):
        made = self.coming[id(ref)][part]
        if made is not None:
            made.wait()
            self.coming[id(ref)][part] = None

    def done(self, ref, index=None):
        target, sent = self.going[id(ref)]
        if index is None:
            sent.append(self.copy(ref, target))
        else:
            sent.append(self.copy(ref.at[index], target.at[index]))

    def close(self, ins, outs):
        for ref in ins:
            for part in range(len(self.coming[id(ref)])):
                self.need(ref, part)
        for ref in outs:
            if not self.going[id(ref)][1]:
                self.done(ref)
        for ref in outs:
            for made in self.going[id(ref)][1]:
                made.wait()


def call(kernel, out, *arrays, step=None, scratch=(), cost=None, parts=None, pieces=0):
    count, last = len(arrays), len(arrays) + len(out)
    parts = parts or {}
    cuts = [parts.get(i, [None]) for i in range(count)]
    copies = sum(len(cut) for cut in cuts) + len(out) + pieces
    lead = 0 if step is None else 1

    def whole(*refs):
        scalars, refs = refs[:lead], refs[lead:]
        far, near = refs[:last], refs[last : 2 * last]
        io = Moves(refs[-1])
        for ref, cut in zip(near[:count], cuts):
            io.coming[id(ref)] = [None] * len(cut)
        for step in range(max(len(cut) for cut in cuts)):
            for source, ref, cut in zip(far[:count], near[:count], cuts):
                if step < len(cut):
                    at = cut[step]
                    pair = (source, ref) if at is None else (source.at[at], ref.at[at])
                    io.coming[id(ref)][step] = io.copy(*pair)
        for target, ref in zip(far[count:], near[count:]):
            io.going[id(ref)] = (target, [])
        kernel(io, *scalars, *near, *refs[2 * last : -1])
        io.close(near[:count], near[count:])

    near = [pltpu.VMEM(array.shape, array.dtype) for array in arrays]
    near += [pltpu.VMEM(shape, kind) for shape, kind in out]
    return pl.pallas_call(
        whole,
        out_shape=[jax.ShapeDtypeStruct(shape, kind) for shape, kind in out],
        in_specs=[SMEM] * lead + [ANY] * count,
        out_specs=[ANY] * len(out),
        scratch_shapes=near
        + [pltpu.VMEM(shape, kind) for shape, kind in scratch]
        + [pltpu.SemaphoreType.DMA((copies,))],
        compiler_params=pltpu.CompilerParams(vmem_limit_bytes=62 * 1024 * 1024),
        cost_estimate=cost,
        name=kernel.__name__,
    )(*([] if step is None else [step]), *arrays)


LIGHT = pl.CostEstimate(flops=1000, transcendentals=0, bytes_accessed=1000)


def nn(a, b):
    return lax.dot_general(a, b, (((1,), (0,)), ((), ())), preferred_element_type=F32)


def nt(a, b):
    return lax.dot_general(a, b, (((1,), (1,)), ((), ())), preferred_element_type=F32)


def tn(a, b):
    return lax.dot_general(a, b, (((0,), (0,)), ((), ())), preferred_element_type=F32)


def iota(shape, dim):
    return lax.broadcasted_iota(jnp.int32, shape, dim)


def one_hot(test):
    return jnp.where(test, 1.0, 0.0).astype(BF)


def rest_pick(back):
    shape = (LATE, 2 * REST)
    row, col = iota(shape, 0), iota(shape, 1)
    if back:
        shape = (2 * REST, LATE)
        row, col = iota(shape, 1), iota(shape, 0)
    return one_hot((row & 3) + 4 * (row >> 3) + REST * ((row >> 2) & 1) == col)


def pack_frame(rows, out_ref, at):
    out_ref[:, at : at + D] = rows[:LATE]
    low = rows[LATE:, :W]
    high = jnp.concatenate([rows[LATE:, W:], jnp.zeros((REST, 2 * W - D), BF)], axis=1)
    both = jnp.concatenate([low, high], axis=0)
    out_ref[:, at + D : at + PACK] = nn(rest_pick(False), both).astype(BF)


def unpack_frame(got_ref):
    both = nn(rest_pick(True), got_ref[:, D:])
    rest = jnp.concatenate([both[:REST], both[REST:, : D - W]], axis=1).astype(BF)
    return got_ref[:, :D], rest


def patch_pick():
    shape = (LATE, LATE)
    row, col = iota(shape, 0), iota(shape, 1)
    return one_hot((row & 31) * 8 + (row >> 5) == col)


def unpack_patches(got_ref, pick, at):
    first = nn(pick, got_ref[:, at : at + D])
    rest = nn(pick, got_ref[:, at + D : at + PACK])
    rest = jnp.concatenate([rest[:REST], rest[REST:, : D - W]], axis=1)
    return jnp.concatenate([first, rest], axis=0).astype(BF)


def pack_patches(rows, pick, out_ref):
    out_ref[:, :D] = tn(pick, rows[:LATE]).astype(BF)
    low = rows[LATE:, :W]
    high = jnp.concatenate([rows[LATE:, W:], jnp.zeros((REST, 2 * W - D), BF)], axis=1)
    out_ref[:, D:] = tn(pick, jnp.concatenate([low, high], axis=0)).astype(BF)


def head_window(head):
    first = head * E // 128 * 128
    last = -(-(head + 1) * E // 128) * 128
    lane = iota((1, last - first), 1) + first
    keep = one_hot((lane >= head * E) & (lane < (head + 1) * E))
    return slice(first, last), keep


def frame_marks(mask_ref):
    row = mask_ref[pl.ds(lax.axis_index("seq"), 1), :].astype(F32)
    return jnp.transpose(jnp.broadcast_to(row, (128, N)))


def patch_marks(mask_ref):
    rank = lax.axis_index("seq")
    shape = (N, F)
    spread = nn(one_hot((iota(shape, 0) & 31) == iota(shape, 1)), mask_ref[...].astype(F32).astype(BF))
    place = iota((N, N), 0) >> 5
    patch = jnp.where(place < 8, rank * 8 + place, LATE + rank * 4 + place - 8)
    chosen = jnp.where(patch == iota((N, N), 1), spread, 0.0)
    return jnp.broadcast_to(jnp.sum(chosen, axis=1, keepdims=True), (N, 128))


def modulation(mod_ref, step, row, marks, rows):
    clean = mod_ref[row, 0:1, :]
    noised = mod_ref[row, pl.ds(step, 1), :]
    wide = jnp.concatenate([marks[rows]] * (D // 128), axis=1)
    return jnp.where(wide == 1.0, clean, noised)


def chunks(size):
    return [slice(i, i + size) for i in range(0, N, size)]


def normalize(x):
    centered = x - jnp.mean(x, axis=1, keepdims=True)
    inverse = lax.rsqrt(jnp.mean(centered * centered, axis=1, keepdims=True) + 1e-06)
    return centered * inverse, inverse


def project(normed, w_ref, q_ref, k_ref, v_ref):
    for i, ref in enumerate((q_ref, k_ref, v_ref)):
        ref[:, :HD] = nt(normed, w_ref[HD * i : HD * i + HD, :]).astype(BF)
        ref[:, HD:] = jnp.zeros((N, W - HD), BF)


class Blocks:
    def __init__(self):
        self.parts = [[] for _ in range(W // 128)]

    def add(self, lanes, value):
        for i in range((lanes.stop - lanes.start) // 128):
            self.parts[lanes.start // 128 + i].append(value[:, 128 * i : 128 * i + 128])

    def join(self):
        return jnp.concatenate([sum(parts[1:], parts[0]) for parts in self.parts], axis=1)


def batches(groups, batch):
    units = [(i, head, *head_window(head)) for i in range(len(groups)) for head in range(H)]
    return [units[i : i + batch] for i in range(0, len(units), batch)]


def attend(q_ref, k_ref, v_ref, probs_ref, heads_ref, groups, batch, same=None):
    heads = [Blocks() for _ in groups]
    for units in batches(groups, batch):
        scores = []
        for i, _, lanes, keep in units:
            scores.append(nt(k_ref[groups[i], lanes], q_ref[groups[i], lanes] * keep))
        probs = []
        for score in scores:
            if same is not None:
                score = jnp.where(same, score, -1e30)
            top = jnp.max(score, axis=0, keepdims=True)
            expo = jnp.exp2((score - top) * (SCALE * math.log2(math.e)))
            share = 1.0 / jnp.sum(expo, axis=0, keepdims=True)
            probs.append((expo * share).astype(BF))
        for prob, (i, _, lanes, keep) in zip(probs, units):
            heads[i].add(lanes, tn(prob, v_ref[groups[i], lanes] * keep))
        for prob, (i, head, _, _) in zip(probs, units):
            probs_ref[head, groups[i], :] = prob
    for rows, parts in zip(groups, heads):
        heads_ref[rows, :] = parts.join().astype(BF)


def attend_back(q_ref, k_ref, v_ref, probs_ref, dheads_ref, dqkv_ref, groups, batch):
    sums = [(Blocks(), Blocks(), Blocks()) for _ in groups]
    for units in batches(groups, batch):
        dheads = [dheads_ref[groups[i], lanes] * keep for i, _, lanes, keep in units]
        dprobs = []
        for dhead, (i, _, lanes, _) in zip(dheads, units):
            dprobs.append(nt(v_ref[groups[i], lanes], dhead))
        dscores = []
        for dprob, (i, head, _, _) in zip(dprobs, units):
            wide = probs_ref[head, groups[i], :].astype(F32)
            total = jnp.sum(wide * dprob, axis=0, keepdims=True)
            dscores.append((wide * (dprob - total)).astype(BF))
        for dhead, dscore, (i, head, lanes, keep) in zip(dheads, dscores, units):
            dq, dk, dv = sums[i]
            dv.add(lanes, nn(probs_ref[head, groups[i], :], dhead))
            dk.add(lanes, nn(dscore, q_ref[groups[i], lanes] * keep))
            dq.add(lanes, tn(dscore, k_ref[groups[i], lanes] * keep))
    for rows, (dq, dk, dv) in zip(groups, sums):
        query, low = dq.join() * SCALE, pltpu.roll(dk.join() * SCALE, W - HD, 1)
        dqkv_ref[rows, : W - 128] = query[:, : W - 128].astype(BF)
        dqkv_ref[rows, W - 128 : W] = (query[:, W - 128 :] + low[:, :128]).astype(BF)
        dqkv_ref[rows, W : 2 * HD] = low[:, 128:].astype(BF)
        dqkv_ref[rows, 2 * HD :] = dv.join().astype(BF)


def split_halves(dqkv_ref, dattn_ref, keep_ref, send_ref):
    core = lax.axis_index("dp") & 1

    def take(ref, side):
        ref[:, :GQ] = dqkv_ref[:, GQ * side : GQ * side + GQ]
        ref[:, GQ:] = dattn_ref[:, GO * side : GO * side + GO]

    @pl.when(core == 0)
    def _():
        take(keep_ref, 0)
        take(send_ref, 1)

    @pl.when(core == 1)
    def _():
        take(keep_ref, 1)
        take(send_ref, 0)


def gated(dout_ref, mod_ref, step, row, marks, dattn_ref):
    for rows in chunks(128):
        gate = modulation(mod_ref, step, row, marks, rows)
        dattn_ref[rows, :D] = (dout_ref[rows, :].astype(F32) * gate).astype(BF)
    dattn_ref[:, D:] = jnp.zeros((N, 2 * GO - D), BF)


def input_gradient(x_ref, dout_ref, dnormed_ref, mod_ref, step, row, marks, out_ref):
    for rows in chunks(128):
        xhat, inverse = normalize(x_ref[rows, :].astype(F32))
        scale = 1.0 + modulation(mod_ref, step, row, marks, rows)
        dxhat = dnormed_ref[rows, :] * scale
        first = jnp.mean(dxhat, axis=1, keepdims=True)
        second = jnp.mean(dxhat * xhat, axis=1, keepdims=True)
        line = inverse * (dxhat - first - xhat * second)
        out_ref[rows, :] = (dout_ref[rows, :].astype(F32) + line).astype(out_ref.dtype)


def norm_rows(x_ref, mod_ref, step, row, marks, normed_ref):
    for rows in chunks(128):
        xhat, _ = normalize(x_ref[rows, :].astype(F32))
        shift = modulation(mod_ref, step, row, marks, rows)
        scale = modulation(mod_ref, step, row + 1, marks, rows)
        normed_ref[rows, :] = (xhat * (1.0 + scale) + shift).astype(BF)


def spatial_forward(
    io, s_ref, x_ref, mask_ref, mod_ref, wqkv_ref, wo_ref, cot_ref,
    packed_ref, normed_ref, q_ref, k_ref, v_ref, probs_ref, heads_ref, mid,
):
    step = s_ref[0]
    io.need(mask_ref)
    marks = frame_marks(mask_ref)
    io.need(x_ref)
    io.need(mod_ref)
    norm_rows(x_ref, mod_ref, step, 0, marks, normed_ref)
    io.done(normed_ref)
    io.need(wqkv_ref)
    project(normed_ref[...], wqkv_ref, q_ref, k_ref, v_ref)
    for ref in (q_ref, k_ref, v_ref):
        io.done(ref)
    attend(q_ref, k_ref, v_ref, probs_ref, heads_ref, [slice(0, N)], 4)
    io.done(probs_ref)
    io.done(heads_ref)
    io.need(cot_ref)
    pack_frame(cot_ref[...], packed_ref, PACK)
    io.need(wo_ref)
    attn = nn(heads_ref[:, :HD], wo_ref[...])
    for rows in chunks(128):
        gate = modulation(mod_ref, step, 2, marks, rows)
        mid[rows, :] = (x_ref[rows, :].astype(F32) + gate * attn[rows]).astype(BF)
    pack_frame(mid[...], packed_ref, 0)


def temporal(
    io, s_ref, got_ref, mask_ref, mod_ref, wqkv_ref, wo_ref,
    packed_ref, normed_ref, heads_ref, keep_ref, send_ref,
    x, dout, q, k, v, probs, dqkv, dattn, dheads, dnormed, dmid,
):
    step = s_ref[0]
    io.need(mask_ref)
    marks = patch_marks(mask_ref)
    pick = patch_pick()
    io.need(got_ref)
    x[...] = unpack_patches(got_ref, pick, 0)
    io.need(mod_ref)
    norm_rows(x, mod_ref, step, 3, marks, normed_ref)
    io.done(normed_ref)
    io.need(wqkv_ref)
    project(normed_ref[...], wqkv_ref, q, k, v)
    groups = chunks(128)
    same = (iota((128, 128), 0) >> 5) == (iota((128, 128), 1) >> 5)
    attend(q, k, v, probs, heads_ref, groups, 3 * H, same)
    io.done(heads_ref)
    dout[...] = unpack_patches(got_ref, pick, PACK)
    gated(dout, mod_ref, step, 5, marks, dattn)
    io.need(wo_ref)
    dheads[:, :HD] = nt(dattn[:, :D], wo_ref[...]).astype(BF)
    dheads[:, HD:] = jnp.zeros((N, W - HD), BF)
    attend_back(q, k, v, probs, dheads, dqkv, groups, 3 * H)
    split_halves(dqkv, dattn, keep_ref, send_ref)
    io.done(send_ref)
    io.done(keep_ref)
    dnormed[...] = nn(dqkv[:, : 3 * HD], wqkv_ref[...])
    input_gradient(x, dout, dnormed, mod_ref, step, 4, marks, dmid)
    pack_patches(dmid[...], pick, packed_ref)


def spatial_back(
    io, s_ref, got_ref, mask_ref, mod_ref, wo_ref, v_ref, probs_ref, q_ref, k_ref,
    dmid_ref, dqkv_ref, keep_ref, send_ref, dattn, dheads,
):
    io.need(mask_ref)
    marks = frame_marks(mask_ref)
    io.need(got_ref)
    first, rest = unpack_frame(got_ref)
    dmid_ref[:LATE, :] = first
    dmid_ref[LATE:, :] = rest
    io.done(dmid_ref)
    io.need(mod_ref)
    gated(dmid_ref, mod_ref, s_ref[0], 2, marks, dattn)
    io.need(wo_ref)
    dheads[:, :HD] = nt(dattn[:, :D], wo_ref[...]).astype(BF)
    dheads[:, HD:] = jnp.zeros((N, W - HD), BF)
    for ref in (v_ref, probs_ref, q_ref, k_ref):
        io.need(ref)
    attend_back(q_ref, k_ref, v_ref, probs_ref, dheads, dqkv_ref, [slice(0, N)], 4)
    io.done(dqkv_ref)
    split_halves(dqkv_ref, dattn, keep_ref, send_ref)


def spatial_input(io, s_ref, dqkv_ref, wqkv_ref, dmid_ref, x_ref, mask_ref, mod_ref, out_ref, dnormed):
    io.need(dqkv_ref)
    io.need(wqkv_ref)
    dnormed[...] = nn(dqkv_ref[:, : 3 * HD], wqkv_ref[...])
    for ref in (dmid_ref, x_ref, mask_ref, mod_ref):
        io.need(ref)
    marks = frame_marks(mask_ref)
    input_gradient(x_ref, dmid_ref, dnormed, mod_ref, s_ref[0], 1, marks, out_ref)


def turn(normed_ref, heads_ref, out_ref, wide, tall):
    wide[:D, :] = jnp.transpose(normed_ref[...].astype(F32))
    wide[D:, :] = jnp.zeros((8, N), F32)
    tall[:W, :] = jnp.transpose(heads_ref[...].astype(F32))
    tall[W:, :] = jnp.zeros((8, N), F32)
    place = iota((8, N), 0)
    for i in range(0, F, 2):
        fours, twos = [], []
        for j in (i, i + 1):
            out_ref[32 * j : 32 * j + 32, :] = wide[36 * j : 36 * j + 32, :].astype(BF)
            out_ref[1280 + 16 * j : 1296 + 16 * j, :] = tall[18 * j : 18 * j + 16, :].astype(BF)
            base = 36 * j + 32
            fours.append(jnp.where(place < 4, wide[base : base + 8, :], wide[base - 4 : base + 4, :]))
            base = 18 * j + 16
            two = tall[base : base + 8, :]
            for shift in (2, 4, 6):
                two = jnp.where(place < shift, two, tall[base - shift : base - shift + 8, :])
            twos.append(two)
        out_ref[1024 + 8 * i : 1040 + 8 * i, :] = jnp.concatenate(fours, axis=0).astype(BF)
        out_ref[1792 + 8 * i : 1808 + 8 * i, :] = jnp.concatenate(twos, axis=0).astype(BF)


def turn_spatial(io, normed_ref, heads_ref, out_ref, wide, tall):
    io.need(normed_ref)
    io.need(heads_ref)
    turn(normed_ref, heads_ref, out_ref, wide, tall)


def turn_temporal(
    io, normed_ref, heads_ref, normed_other_ref, heads_other_ref, own_ref, other_ref, wide, tall
):
    io.need(normed_ref)
    io.need(heads_ref)
    turn(normed_ref, heads_ref, own_ref, wide, tall)
    io.done(own_ref)
    io.need(normed_other_ref)
    io.need(heads_other_ref)
    turn(normed_other_ref, heads_other_ref, other_ref, wide, tall)


SHARE_PARTS = {
    0: [(slice(1280, 2048), slice(None)), (slice(0, 1280), slice(None))],
    1: [(slice(1280, 2048), slice(None)), (slice(0, 1280), slice(None))],
    2: [(slice(None), slice(GQ, GQ + GO)), (slice(None), slice(0, GQ))],
    3: [(slice(None), slice(GQ, GQ + GO)), (slice(None), slice(0, GQ))],
}


def weight_shares(io, a_ref, b_ref, keep_ref, got_ref, out_ref):
    def both(rows):
        return jnp.concatenate([a_ref[rows, :], b_ref[rows, :]], axis=1)

    def pair(lanes):
        return jnp.concatenate([keep_ref[:, lanes], got_ref[:, lanes]], axis=0)

    def send(start, size):
        io.done(out_ref, (slice(None), slice(start, start + size), slice(None)))

    place = iota((F * 8, 128), 0) & 7
    for ref in (a_ref, b_ref, keep_ref, got_ref):
        io.need(ref, 0)
    main, rest = both(slice(1280, 1792)), both(slice(1792, 2048))
    right = pair(slice(GQ, GQ + GO))
    part, last = nn(main, right).astype(BF), nn(rest, right)
    for j in range(5):
        out_ref[:, 224 + 16 * j : 240 + 16 * j, :] = part[:, 128 * j : 128 * j + 128].reshape(F, 16, 128)
    four = last[:, :128]
    for j in (1, 2, 3):
        four = jnp.where(place < 2 * j, four, last[:, 128 * j : 128 * j + 128])
    both_extra = [four.reshape(F, 8, 128), last[:, 512:].reshape(F, 8, 128)]
    out_ref[:, 336:352, :] = jnp.concatenate(both_extra, axis=1).astype(BF)
    for ref in (a_ref, b_ref, keep_ref, got_ref):
        io.need(ref, 1)
    main, rest = both(slice(0, 1024)), both(slice(1024, 1280))
    extra = []
    for j in range(0, 7, 2):
        lanes = slice(128 * j, min(128 * j + 256, GQ))
        right = pair(lanes)
        part = nn(main, right).astype(BF)
        out_ref[:, 32 * j : 32 * j + 32, :] = part[:, :128].reshape(F, 32, 128)
        last = nn(rest, right)
        if j < 6:
            out_ref[:, 32 * j + 32 : 32 * j + 64, :] = part[:, 128:].reshape(F, 32, 128)
            last = jnp.where(place < 4, last[:, :128], last[:, 128:])
            send(32 * j, 64)
        extra.append(last.reshape(F, 8, 128))
    for j in range(2):
        both_extra = jnp.concatenate(extra[2 * j : 2 * j + 2], axis=1)
        out_ref[:, 304 + 16 * j : 320 + 16 * j, :] = both_extra.astype(BF)
    send(192, 160)


SUM_STARTS = [0, 80, 160, 256, ROWS]
SUM_PARTS = [(slice(None), slice(i, j), slice(None)) for i, j in zip(SUM_STARTS, SUM_STARTS[1:])]


def sum_shares(io, got_ref, out_ref):
    for part in range(4):
        io.need(got_ref, part)
        for start in range(SUM_STARTS[part], SUM_STARTS[part + 1], 16):
            rows = slice(start, start + 16)
            sums = [got_ref[i, rows, :].astype(F32) for i in range(F)]
            while len(sums) > 1:
                sums = [one + two for one, two in zip(sums[::2], sums[1::2])]
            out_ref[rows, :] = sums[0].astype(BF)


def finish(io, own_ref, one_ref, two_ref, three_ref, q_ref, o_ref):
    factor = 1.0 / math.sqrt(4 * F * N)
    for ref in (own_ref, one_ref, two_ref, three_ref):
        io.need(ref)
    own, one, two, three = (ref[...].astype(F32) for ref in (own_ref, one_ref, two_ref, three_ref))
    same, other = (own + two) * factor, (one + three) * factor
    first = (lax.axis_index("dp") & 1) == 0
    halves = [jnp.where(first, same, other), jnp.where(first, other, same)]
    for side, half in enumerate(halves):
        for j in range(7):
            start = GQ * side + 128 * j
            width = min(128, 3 * HD - start)
            q_ref[:32, start : start + width] = half[32 * j : 32 * j + 32, :width]
            base = 304 + 4 * j
            q_ref[32:, start : start + width] = half[base : base + 4, :width]
        for j in range(5):
            start = GO * side + 128 * j
            if start < D:
                o_ref[:16, start : start + 128] = half[224 + 16 * j : 240 + 16 * j, :]
                o_ref[16:, start : start + 128] = half[336 + 2 * j : 338 + 2 * j, :]


def reduce_shares(got):
    own = call(sum_shares, [((ROWS, 128), BF)], got, cost=LIGHT, parts={0: SUM_PARTS})[0]
    two = lax.ppermute(own, "dp", [(0, 2), (1, 3), (2, 0), (3, 1)])
    one, three = over_cores(own), over_cores(two)
    return call(finish, [((36, 3 * HD), F32), ((18, D), F32)], own, one, two, three, cost=LIGHT)


def over_cores(array):
    return lax.ppermute(array, "dp", [(0, 1), (1, 0), (2, 3), (3, 2)])


def exchange(packed):
    shape = packed.shape
    sent = lax.all_to_all(packed.reshape(F, shape[0] // F, shape[1]), "seq", 0, 0, tiled=True)
    return sent.reshape(shape)


def body(tokens, cotangent, mask, t_index, mod_table, wqkv_s, wo_s, wqkv_t, wo_t):
    x, cot, marks = tokens[0, 0], cotangent[0, 0], mask[0]
    mods, wqkv_s, wqkv_t = jnp.transpose(mod_table, (1, 0, 2)), wqkv_s.T, wqkv_t.T
    packed, normed_s, q, k, v, probs, heads_s = call(
        spatial_forward,
        [((LATE, 2 * PACK), BF), ((N, D), BF)] + [((N, W), BF)] * 3 + [((H, N, N), BF), ((N, W), BF)],
        x, marks, mods, wqkv_s, wo_s, cot,
        step=t_index, scratch=[((N, D), BF)],
    )
    got = exchange(packed)
    turn_scratch = [((D + 8, N), F32), ((W + 8, N), F32)]
    turned = [((2048, N), BF)]
    turned_s = call(turn_spatial, turned, normed_s, heads_s, scratch=turn_scratch, cost=LIGHT)[0]
    other_s = over_cores(turned_s)
    got, turned_s = lax.optimization_barrier((got, turned_s))
    halves = [((N, GQ + GO), BF)] * 2
    packed, normed_t, heads_t, keep, send = call(
        temporal,
        [((LATE, PACK), BF), ((N, D), BF), ((N, W), BF)] + halves,
        got, marks, mods, wqkv_t, wo_t,
        step=t_index, scratch=[((N, D), BF)] * 2 + [((N, W), BF)] * 3 + [((H, N, 128), BF)]
        + [((N, PACK), BF), ((N, 2 * GO), BF), ((N, W), BF), ((N, D), F32), ((N, D), BF)],
    )
    got = exchange(packed)
    turned_t, other_t = call(
        turn_temporal, turned * 2,
        normed_t, heads_t, over_cores(normed_t), over_cores(heads_t),
        scratch=turn_scratch, cost=LIGHT,
    )
    shares = [((F, ROWS, 128), BF)]
    shares_t = call(
        weight_shares, shares, turned_t, other_t, keep, over_cores(send),
        cost=LIGHT, parts=SHARE_PARTS, pieces=4,
    )[0]
    got, shares_t = lax.optimization_barrier((got, shares_t))
    shares_t = lax.all_to_all(shares_t, "seq", 0, 0, tiled=True)
    dmid, dqkv, keep, send = call(
        spatial_back,
        [((N, D), BF), ((N, PACK), BF)] + halves,
        got, marks, mods, wo_s, v, probs, q, k,
        step=t_index, scratch=[((N, 2 * GO), BF), ((N, W), BF)],
    )
    shares_s = call(
        weight_shares, shares, turned_s, other_s, keep, over_cores(send),
        parts=SHARE_PARTS, pieces=4,
    )[0]
    shares_t, shares_s = lax.optimization_barrier((shares_t, shares_s))
    shares_s = lax.all_to_all(shares_s, "seq", 0, 0, tiled=True)
    grad = call(
        spatial_input, [((N, D), F32)], dqkv, wqkv_s, dmid, x, marks, mods,
        step=t_index, scratch=[((N, D), F32)], cost=LIGHT,
    )[0]
    grads_t = reduce_shares(shares_t)
    shares_s, grad, *grads_t = lax.optimization_barrier((shares_s, grad, *grads_t))
    return (grad[None, None], *reduce_shares(shares_s), *grads_t)


def solution(mesh):
    return jax.shard_map(
        body,
        mesh=mesh,
        in_specs=(
            P("dp", "seq", None, None),
            P("dp", "seq", None, None),
            P("dp", None, None),
            P("dp"),
            P(),
            P(),
            P(),
            P(),
            P(),
        ),
        out_specs=(
            P("dp", "seq", None, None),
            P("seq", None),
            P("seq", None),
            P("seq", None),
            P("seq", None),
        ),
        check_vma=False,
    )
```

```python
import math

import jax
import jax.numpy as jnp
from jax import lax
from jax.experimental import pallas as pl
from jax.experimental.pallas import tpu as pltpu
from jax.sharding import PartitionSpec as P

D = 1152
H = 8
E = 72
HD = 576
N = 384
F = 32
W = 640
LATE = 256
REST = 128
PACK = 1792
GQ = 896
GO = 640
ROWS = 352
BF = jnp.bfloat16
F32 = jnp.float32
SCALE = E**-0.5
SMEM = pl.BlockSpec(memory_space=pltpu.SMEM)
ANY = pl.BlockSpec(memory_space=pl.ANY)


class Moves:
    def __init__(self, sems):
        self.sems, self.used, self.coming, self.going = sems, 0, {}, {}

    def copy(self, source, target):
        made = pltpu.make_async_copy(source, target, self.sems.at[self.used])
        self.used += 1
        made.start()
        return made

    def need(self, ref, part=0):
        made = self.coming[id(ref)][part]
        if made is not None:
            made.wait()
            self.coming[id(ref)][part] = None

    def done(self, ref, index=None):
        target, sent = self.going[id(ref)]
        if index is None:
            sent.append(self.copy(ref, target))
        else:
            sent.append(self.copy(ref.at[index], target.at[index]))

    def close(self, ins, outs):
        for ref in ins:
            for part in range(len(self.coming[id(ref)])):
                self.need(ref, part)
        for ref in outs:
            if not self.going[id(ref)][1]:
                self.done(ref)
        for ref in outs:
            for made in self.going[id(ref)][1]:
                made.wait()


def call(kernel, out, *arrays, step=None, scratch=(), cost=None, parts=None, pieces=0):
    count, last = len(arrays), len(arrays) + len(out)
    parts = parts or {}
    cuts = [parts.get(i, [None]) for i in range(count)]
    copies = sum(len(cut) for cut in cuts) + len(out) + pieces
    lead = 0 if step is None else 1

    def whole(*refs):
        scalars, refs = refs[:lead], refs[lead:]
        far, near = refs[:last], refs[last : 2 * last]
        io = Moves(refs[-1])
        for ref, cut in zip(near[:count], cuts):
            io.coming[id(ref)] = [None] * len(cut)
        for step in range(max(len(cut) for cut in cuts)):
            for source, ref, cut in zip(far[:count], near[:count], cuts):
                if step < len(cut):
                    at = cut[step]
                    pair = (source, ref) if at is None else (source.at[at], ref.at[at])
                    io.coming[id(ref)][step] = io.copy(*pair)
        for target, ref in zip(far[count:], near[count:]):
            io.going[id(ref)] = (target, [])
        kernel(io, *scalars, *near, *refs[2 * last : -1])
        io.close(near[:count], near[count:])

    near = [pltpu.VMEM(array.shape, array.dtype) for array in arrays]
    near += [pltpu.VMEM(shape, kind) for shape, kind in out]
    return pl.pallas_call(
        whole,
        out_shape=[jax.ShapeDtypeStruct(shape, kind) for shape, kind in out],
        in_specs=[SMEM] * lead + [ANY] * count,
        out_specs=[ANY] * len(out),
        scratch_shapes=near
        + [pltpu.VMEM(shape, kind) for shape, kind in scratch]
        + [pltpu.SemaphoreType.DMA((copies,))],
        compiler_params=pltpu.CompilerParams(vmem_limit_bytes=(62 * 1024 + 400) * 1024),
        cost_estimate=cost,
        name=kernel.__name__,
    )(*([] if step is None else [step]), *arrays)


LIGHT = pl.CostEstimate(flops=1000, transcendentals=0, bytes_accessed=1000)


def nn(a, b):
    return lax.dot_general(a, b, (((1,), (0,)), ((), ())), preferred_element_type=F32)


def nt(a, b):
    return lax.dot_general(a, b, (((1,), (1,)), ((), ())), preferred_element_type=F32)


def tn(a, b):
    return lax.dot_general(a, b, (((0,), (0,)), ((), ())), preferred_element_type=F32)


def iota(shape, dim):
    return lax.broadcasted_iota(jnp.int32, shape, dim)


def one_hot(test):
    return jnp.where(test, 1.0, 0.0).astype(BF)


def rest_pick(back):
    shape = (LATE, 2 * REST)
    row, col = iota(shape, 0), iota(shape, 1)
    if back:
        shape = (2 * REST, LATE)
        row, col = iota(shape, 1), iota(shape, 0)
    return one_hot((row & 3) + 4 * (row >> 3) + REST * ((row >> 2) & 1) == col)


def pack_frame(rows, out_ref, at):
    out_ref[:, at : at + D] = rows[:LATE]
    low = rows[LATE:, :W]
    high = jnp.concatenate([rows[LATE:, W:], jnp.zeros((REST, 2 * W - D), BF)], axis=1)
    both = jnp.concatenate([low, high], axis=0)
    out_ref[:, at + D : at + PACK] = nn(rest_pick(False), both).astype(BF)


def unpack_frame(got_ref):
    both = nn(rest_pick(True), got_ref[:, D:])
    rest = jnp.concatenate([both[:REST], both[REST:, : D - W]], axis=1).astype(BF)
    return got_ref[:, :D], rest


def patch_pick():
    shape = (LATE, LATE)
    row, col = iota(shape, 0), iota(shape, 1)
    return one_hot((row & 31) * 8 + (row >> 5) == col)


def unpack_patches(got_ref, pick, at):
    first = nn(pick, got_ref[:, at : at + D])
    rest = nn(pick, got_ref[:, at + D : at + PACK])
    rest = jnp.concatenate([rest[:REST], rest[REST:, : D - W]], axis=1)
    return jnp.concatenate([first, rest], axis=0).astype(BF)


def pack_patches(rows, pick, out_ref):
    out_ref[:, :D] = tn(pick, rows[:LATE]).astype(BF)
    low = rows[LATE:, :W]
    high = jnp.concatenate([rows[LATE:, W:], jnp.zeros((REST, 2 * W - D), BF)], axis=1)
    out_ref[:, D:] = tn(pick, jnp.concatenate([low, high], axis=0)).astype(BF)


def head_window(head):
    first = head * E // 128 * 128
    last = -(-(head + 1) * E // 128) * 128
    lane = iota((1, last - first), 1) + first
    keep = one_hot((lane >= head * E) & (lane < (head + 1) * E))
    return slice(first, last), keep


def frame_marks(mask_ref):
    row = mask_ref[pl.ds(lax.axis_index("seq"), 1), :].astype(F32)
    return jnp.transpose(jnp.broadcast_to(row, (128, N)))


def patch_marks(mask_ref):
    rank = lax.axis_index("seq")
    shape = (N, F)
    spread = nn(one_hot((iota(shape, 0) & 31) == iota(shape, 1)), mask_ref[...].astype(F32).astype(BF))
    place = iota((N, N), 0) >> 5
    patch = jnp.where(place < 8, rank * 8 + place, LATE + rank * 4 + place - 8)
    chosen = jnp.where(patch == iota((N, N), 1), spread, 0.0)
    return jnp.broadcast_to(jnp.sum(chosen, axis=1, keepdims=True), (N, 128))


def modulation(mod_ref, step, row, marks, rows):
    clean = mod_ref[row, 0:1, :]
    noised = mod_ref[row, pl.ds(step, 1), :]
    wide = jnp.concatenate([marks[rows]] * (D // 128), axis=1)
    return jnp.where(wide == 1.0, clean, noised)


def chunks(size):
    return [slice(i, i + size) for i in range(0, N, size)]


def normalize(x):
    centered = x - jnp.mean(x, axis=1, keepdims=True)
    inverse = lax.rsqrt(jnp.mean(centered * centered, axis=1, keepdims=True) + 1e-06)
    return centered * inverse, inverse


def project(normed, w_ref, q_ref, k_ref, v_ref):
    for i, ref in enumerate((q_ref, k_ref, v_ref)):
        ref[:, :HD] = nt(normed, w_ref[HD * i : HD * i + HD, :]).astype(BF)
        ref[:, HD:] = jnp.zeros((N, W - HD), BF)


class Blocks:
    def __init__(self):
        self.parts = [[] for _ in range(W // 128)]

    def add(self, lanes, value):
        for i in range((lanes.stop - lanes.start) // 128):
            self.parts[lanes.start // 128 + i].append(value[:, 128 * i : 128 * i + 128])

    def join(self):
        return jnp.concatenate([sum(parts[1:], parts[0]) for parts in self.parts], axis=1)


def batches(groups, batch):
    units = [(i, head, *head_window(head)) for i in range(len(groups)) for head in range(H)]
    return [units[i : i + batch] for i in range(0, len(units), batch)]


def attend(q_ref, k_ref, v_ref, probs_ref, heads_ref, groups, batch, same=None):
    heads = [Blocks() for _ in groups]
    for units in batches(groups, batch):
        scores = []
        for i, _, lanes, keep in units:
            scores.append(nt(k_ref[groups[i], lanes], q_ref[groups[i], lanes] * keep))
        probs = []
        for score in scores:
            if same is not None:
                score = jnp.where(same, score, -1e30)
            top = jnp.max(score, axis=0, keepdims=True)
            expo = jnp.exp2((score - top) * (SCALE * math.log2(math.e)))
            share = 1.0 / jnp.sum(expo, axis=0, keepdims=True)
            probs.append((expo * share).astype(BF))
        for prob, (i, _, lanes, keep) in zip(probs, units):
            heads[i].add(lanes, tn(prob, v_ref[groups[i], lanes] * keep))
        for prob, (i, head, _, _) in zip(probs, units):
            probs_ref[head, groups[i], :] = prob
    for rows, parts in zip(groups, heads):
        heads_ref[rows, :] = parts.join().astype(BF)


def attend_back(q_ref, k_ref, v_ref, probs_ref, dheads_ref, dqkv_ref, groups, batch):
    sums = [(Blocks(), Blocks(), Blocks()) for _ in groups]
    for units in batches(groups, batch):
        dheads = [dheads_ref[groups[i], lanes] * keep for i, _, lanes, keep in units]
        dprobs = []
        for dhead, (i, _, lanes, _) in zip(dheads, units):
            dprobs.append(nt(v_ref[groups[i], lanes], dhead))
        dscores = []
        for dprob, (i, head, _, _) in zip(dprobs, units):
            wide = probs_ref[head, groups[i], :].astype(F32)
            total = jnp.sum(wide * dprob, axis=0, keepdims=True)
            dscores.append((wide * (dprob - total)).astype(BF))
        for dhead, dscore, (i, head, lanes, keep) in zip(dheads, dscores, units):
            dq, dk, dv = sums[i]
            dv.add(lanes, nn(probs_ref[head, groups[i], :], dhead))
            dk.add(lanes, nn(dscore, q_ref[groups[i], lanes] * keep))
            dq.add(lanes, tn(dscore, k_ref[groups[i], lanes] * keep))
    for rows, (dq, dk, dv) in zip(groups, sums):
        query, low = dq.join() * SCALE, pltpu.roll(dk.join() * SCALE, W - HD, 1)
        dqkv_ref[rows, : W - 128] = query[:, : W - 128].astype(BF)
        dqkv_ref[rows, W - 128 : W] = (query[:, W - 128 :] + low[:, :128]).astype(BF)
        dqkv_ref[rows, W : 2 * HD] = low[:, 128:].astype(BF)
        dqkv_ref[rows, 2 * HD :] = dv.join().astype(BF)


def split_halves(dqkv_ref, dattn_ref, keep_ref, send_ref):
    core = lax.axis_index("dp") & 1

    def take(ref, side):
        ref[:, :GQ] = dqkv_ref[:, GQ * side : GQ * side + GQ]
        ref[:, GQ:] = dattn_ref[:, GO * side : GO * side + GO]

    @pl.when(core == 0)
    def _():
        take(keep_ref, 0)
        take(send_ref, 1)

    @pl.when(core == 1)
    def _():
        take(keep_ref, 1)
        take(send_ref, 0)


def gated(dout_ref, mod_ref, step, row, marks, dattn_ref):
    for rows in chunks(128):
        gate = modulation(mod_ref, step, row, marks, rows)
        dattn_ref[rows, :D] = (dout_ref[rows, :].astype(F32) * gate).astype(BF)
    dattn_ref[:, D:] = jnp.zeros((N, 2 * GO - D), BF)


def input_gradient(x_ref, dout_ref, dnormed_ref, mod_ref, step, row, marks, out_ref):
    for rows in chunks(128):
        xhat, inverse = normalize(x_ref[rows, :].astype(F32))
        scale = 1.0 + modulation(mod_ref, step, row, marks, rows)
        dxhat = dnormed_ref[rows, :] * scale
        first = jnp.mean(dxhat, axis=1, keepdims=True)
        second = jnp.mean(dxhat * xhat, axis=1, keepdims=True)
        line = inverse * (dxhat - first - xhat * second)
        out_ref[rows, :] = (dout_ref[rows, :].astype(F32) + line).astype(out_ref.dtype)


def norm_rows(x_ref, mod_ref, step, row, marks, normed_ref):
    for rows in chunks(128):
        xhat, _ = normalize(x_ref[rows, :].astype(F32))
        shift = modulation(mod_ref, step, row, marks, rows)
        scale = modulation(mod_ref, step, row + 1, marks, rows)
        normed_ref[rows, :] = (xhat * (1.0 + scale) + shift).astype(BF)


def spatial_forward(
    io, s_ref, x_ref, mask_ref, mod_ref, wqkv_ref, wo_ref, cot_ref,
    packed_ref, normed_ref, q_ref, k_ref, v_ref, probs_ref, heads_ref, mid,
):
    step = s_ref[0]
    io.need(mask_ref)
    marks = frame_marks(mask_ref)
    io.need(x_ref)
    io.need(mod_ref)
    norm_rows(x_ref, mod_ref, step, 0, marks, normed_ref)
    io.done(normed_ref)
    io.need(wqkv_ref)
    project(normed_ref[...], wqkv_ref, q_ref, k_ref, v_ref)
    for ref in (q_ref, k_ref, v_ref):
        io.done(ref)
    attend(q_ref, k_ref, v_ref, probs_ref, heads_ref, [slice(0, N)], 4)
    io.done(probs_ref)
    io.done(heads_ref)
    io.need(cot_ref)
    pack_frame(cot_ref[...], packed_ref, PACK)
    io.need(wo_ref)
    attn = nn(heads_ref[:, :HD], wo_ref[...])
    for rows in chunks(128):
        gate = modulation(mod_ref, step, 2, marks, rows)
        mid[rows, :] = (x_ref[rows, :].astype(F32) + gate * attn[rows]).astype(BF)
    pack_frame(mid[...], packed_ref, 0)


def temporal(
    io, s_ref, got_ref, mask_ref, mod_ref, wqkv_ref, wo_ref,
    packed_ref, normed_ref, heads_ref, keep_ref, send_ref,
    x, dout, q, k, v, probs, dqkv, dattn, dheads, dnormed, dmid,
):
    step = s_ref[0]
    io.need(mask_ref)
    marks = patch_marks(mask_ref)
    pick = patch_pick()
    io.need(got_ref)
    x[...] = unpack_patches(got_ref, pick, 0)
    io.need(mod_ref)
    norm_rows(x, mod_ref, step, 3, marks, normed_ref)
    io.done(normed_ref)
    io.need(wqkv_ref)
    project(normed_ref[...], wqkv_ref, q, k, v)
    groups = chunks(128)
    same = (iota((128, 128), 0) >> 5) == (iota((128, 128), 1) >> 5)
    attend(q, k, v, probs, heads_ref, groups, 3 * H, same)
    io.done(heads_ref)
    dout[...] = unpack_patches(got_ref, pick, PACK)
    gated(dout, mod_ref, step, 5, marks, dattn)
    io.need(wo_ref)
    dheads[:, :HD] = nt(dattn[:, :D], wo_ref[...]).astype(BF)
    dheads[:, HD:] = jnp.zeros((N, W - HD), BF)
    attend_back(q, k, v, probs, dheads, dqkv, groups, 3 * H)
    split_halves(dqkv, dattn, keep_ref, send_ref)
    io.done(send_ref)
    io.done(keep_ref)
    dnormed[...] = nn(dqkv[:, : 3 * HD], wqkv_ref[...])
    input_gradient(x, dout, dnormed, mod_ref, step, 4, marks, dmid)
    pack_patches(dmid[...], pick, packed_ref)


def spatial_back(
    io, s_ref, got_ref, mask_ref, mod_ref, wo_ref, v_ref, probs_ref, q_ref, k_ref,
    dmid_ref, dqkv_ref, keep_ref, send_ref, dattn, dheads,
):
    io.need(mask_ref)
    marks = frame_marks(mask_ref)
    io.need(got_ref)
    first, rest = unpack_frame(got_ref)
    dmid_ref[:LATE, :] = first
    dmid_ref[LATE:, :] = rest
    io.done(dmid_ref)
    io.need(mod_ref)
    gated(dmid_ref, mod_ref, s_ref[0], 2, marks, dattn)
    io.need(wo_ref)
    dheads[:, :HD] = nt(dattn[:, :D], wo_ref[...]).astype(BF)
    dheads[:, HD:] = jnp.zeros((N, W - HD), BF)
    for ref in (v_ref, probs_ref, q_ref, k_ref):
        io.need(ref)
    attend_back(q_ref, k_ref, v_ref, probs_ref, dheads, dqkv_ref, [slice(0, N)], 4)
    io.done(dqkv_ref)
    split_halves(dqkv_ref, dattn, keep_ref, send_ref)


def spatial_input(io, s_ref, dqkv_ref, wqkv_ref, dmid_ref, x_ref, mask_ref, mod_ref, out_ref, dnormed):
    io.need(dqkv_ref)
    io.need(wqkv_ref)
    dnormed[...] = nn(dqkv_ref[:, : 3 * HD], wqkv_ref[...])
    for ref in (dmid_ref, x_ref, mask_ref, mod_ref):
        io.need(ref)
    marks = frame_marks(mask_ref)
    input_gradient(x_ref, dmid_ref, dnormed, mod_ref, s_ref[0], 1, marks, out_ref)


def turn(normed_ref, heads_ref, out_ref, wide, tall):
    wide[:D, :] = jnp.transpose(normed_ref[...].astype(F32))
    wide[D:, :] = jnp.zeros((8, N), F32)
    tall[:W, :] = jnp.transpose(heads_ref[...].astype(F32))
    tall[W:, :] = jnp.zeros((8, N), F32)
    place = iota((8, N), 0)
    for i in range(0, F, 2):
        fours, twos = [], []
        for j in (i, i + 1):
            out_ref[32 * j : 32 * j + 32, :] = wide[36 * j : 36 * j + 32, :].astype(BF)
            out_ref[1280 + 16 * j : 1296 + 16 * j, :] = tall[18 * j : 18 * j + 16, :].astype(BF)
            base = 36 * j + 32
            fours.append(jnp.where(place < 4, wide[base : base + 8, :], wide[base - 4 : base + 4, :]))
            base = 18 * j + 16
            two = tall[base : base + 8, :]
            for shift in (2, 4, 6):
                two = jnp.where(place < shift, two, tall[base - shift : base - shift + 8, :])
            twos.append(two)
        out_ref[1024 + 8 * i : 1040 + 8 * i, :] = jnp.concatenate(fours, axis=0).astype(BF)
        out_ref[1792 + 8 * i : 1808 + 8 * i, :] = jnp.concatenate(twos, axis=0).astype(BF)


def turn_spatial(io, normed_ref, heads_ref, out_ref, wide, tall):
    io.need(normed_ref)
    io.need(heads_ref)
    turn(normed_ref, heads_ref, out_ref, wide, tall)


def turn_temporal(
    io, normed_ref, heads_ref, normed_other_ref, heads_other_ref, own_ref, other_ref, wide, tall
):
    io.need(normed_ref)
    io.need(heads_ref)
    turn(normed_ref, heads_ref, own_ref, wide, tall)
    io.done(own_ref)
    io.need(normed_other_ref)
    io.need(heads_other_ref)
    turn(normed_other_ref, heads_other_ref, other_ref, wide, tall)


SHARE_PARTS = {
    0: [(slice(1280, 2048), slice(None)), (slice(0, 1280), slice(None))],
    1: [(slice(1280, 2048), slice(None)), (slice(0, 1280), slice(None))],
    2: [(slice(None), slice(GQ, GQ + GO)), (slice(None), slice(0, GQ))],
    3: [(slice(None), slice(GQ, GQ + GO)), (slice(None), slice(0, GQ))],
}


def weight_shares(io, a_ref, b_ref, keep_ref, got_ref, out_ref):
    def both(rows):
        return jnp.concatenate([a_ref[rows, :], b_ref[rows, :]], axis=1)

    def pair(lanes):
        return jnp.concatenate([keep_ref[:, lanes], got_ref[:, lanes]], axis=0)

    def send(start, size):
        io.done(out_ref, (slice(None), slice(start, start + size), slice(None)))

    place = iota((F * 8, 128), 0) & 7
    for ref in (a_ref, b_ref, keep_ref, got_ref):
        io.need(ref, 0)
    main, rest = both(slice(1280, 1792)), both(slice(1792, 2048))
    right = pair(slice(GQ, GQ + GO))
    part, last = nn(main, right).astype(BF), nn(rest, right)
    for j in range(5):
        out_ref[:, 224 + 16 * j : 240 + 16 * j, :] = part[:, 128 * j : 128 * j + 128].reshape(F, 16, 128)
    four = last[:, :128]
    for j in (1, 2, 3):
        four = jnp.where(place < 2 * j, four, last[:, 128 * j : 128 * j + 128])
    both_extra = [four.reshape(F, 8, 128), last[:, 512:].reshape(F, 8, 128)]
    out_ref[:, 336:352, :] = jnp.concatenate(both_extra, axis=1).astype(BF)
    for ref in (a_ref, b_ref, keep_ref, got_ref):
        io.need(ref, 1)
    main, rest = both(slice(0, 1024)), both(slice(1024, 1280))
    extra = []
    for j in range(0, 7, 2):
        lanes = slice(128 * j, min(128 * j + 256, GQ))
        right = pair(lanes)
        part = nn(main, right).astype(BF)
        out_ref[:, 32 * j : 32 * j + 32, :] = part[:, :128].reshape(F, 32, 128)
        last = nn(rest, right)
        if j < 6:
            out_ref[:, 32 * j + 32 : 32 * j + 64, :] = part[:, 128:].reshape(F, 32, 128)
            last = jnp.where(place < 4, last[:, :128], last[:, 128:])
            send(32 * j, 64)
        extra.append(last.reshape(F, 8, 128))
    for j in range(2):
        both_extra = jnp.concatenate(extra[2 * j : 2 * j + 2], axis=1)
        out_ref[:, 304 + 16 * j : 320 + 16 * j, :] = both_extra.astype(BF)
    send(192, 160)


SUM_STARTS = [0, 80, 160, 256, ROWS]
SUM_PARTS = [(slice(None), slice(i, j), slice(None)) for i, j in zip(SUM_STARTS, SUM_STARTS[1:])]


def sum_shares(io, got_ref, out_ref):
    for part in range(4):
        io.need(got_ref, part)
        for start in range(SUM_STARTS[part], SUM_STARTS[part + 1], 16):
            rows = slice(start, start + 16)
            sums = [got_ref[i, rows, :].astype(F32) for i in range(F)]
            while len(sums) > 1:
                sums = [one + two for one, two in zip(sums[::2], sums[1::2])]
            out_ref[rows, :] = sums[0].astype(BF)


def place_shares(own, one, two, three, q_ref, o_ref):
    factor = 1.0 / math.sqrt(4 * F * N)
    own, one, two, three = (ref[...].astype(F32) for ref in (own, one, two, three))
    same, other = (own + two) * factor, (one + three) * factor
    first = (lax.axis_index("dp") & 1) == 0
    halves = [jnp.where(first, same, other), jnp.where(first, other, same)]
    for side, half in enumerate(halves):
        for j in range(7):
            start = GQ * side + 128 * j
            width = min(128, 3 * HD - start)
            q_ref[:32, start : start + width] = half[32 * j : 32 * j + 32, :width]
            base = 304 + 4 * j
            q_ref[32:, start : start + width] = half[base : base + 4, :width]
        for j in range(5):
            start = GO * side + 128 * j
            if start < D:
                o_ref[:16, start : start + 128] = half[224 + 16 * j : 240 + 16 * j, :]
                o_ref[16:, start : start + 128] = half[336 + 2 * j : 338 + 2 * j, :]


def finish(io, *refs):
    temporal_refs, spatial_refs, outs = refs[:4], refs[4:8], refs[8:]
    for ref in temporal_refs:
        io.need(ref)
    place_shares(*temporal_refs, *outs[2:])
    for ref in outs[2:]:
        io.done(ref)
    for ref in spatial_refs:
        io.need(ref)
    place_shares(*spatial_refs, *outs[:2])


def sum_seq(got):
    return call(sum_shares, [((ROWS, 128), BF)], got, cost=LIGHT, parts={0: SUM_PARTS})[0]


def over_chips(array):
    return lax.ppermute(array, "dp", [(0, 2), (1, 3), (2, 0), (3, 1)])


def over_cores(array):
    return lax.ppermute(array, "dp", [(0, 1), (1, 0), (2, 3), (3, 2)])


def exchange(packed):
    shape = packed.shape
    sent = lax.all_to_all(packed.reshape(F, shape[0] // F, shape[1]), "seq", 0, 0, tiled=True)
    return sent.reshape(shape)


def body(tokens, cotangent, mask, t_index, mod_table, wqkv_s, wo_s, wqkv_t, wo_t):
    x, cot, marks = tokens[0, 0], cotangent[0, 0], mask[0]
    mods, wqkv_s, wqkv_t = jnp.transpose(mod_table, (1, 0, 2)), wqkv_s.T, wqkv_t.T
    packed, normed_s, q, k, v, probs, heads_s = call(
        spatial_forward,
        [((LATE, 2 * PACK), BF), ((N, D), BF)] + [((N, W), BF)] * 3 + [((H, N, N), BF), ((N, W), BF)],
        x, marks, mods, wqkv_s, wo_s, cot,
        step=t_index, scratch=[((N, D), BF)],
    )
    got = exchange(packed)
    turn_scratch = [((D + 8, N), F32), ((W + 8, N), F32)]
    turned = [((2048, N), BF)]
    turned_s = call(turn_spatial, turned, normed_s, heads_s, scratch=turn_scratch, cost=LIGHT)[0]
    other_s = over_cores(turned_s)
    got, turned_s = lax.optimization_barrier((got, turned_s))
    halves = [((N, GQ + GO), BF)] * 2
    packed, normed_t, heads_t, keep, send = call(
        temporal,
        [((LATE, PACK), BF), ((N, D), BF), ((N, W), BF)] + halves,
        got, marks, mods, wqkv_t, wo_t,
        step=t_index, scratch=[((N, D), BF)] * 2 + [((N, W), BF)] * 3 + [((H, N, 128), BF)]
        + [((N, PACK), BF), ((N, 2 * GO), BF), ((N, W), BF), ((N, D), F32), ((N, D), BF)],
    )
    got = exchange(packed)
    turned_t, other_t = call(
        turn_temporal, turned * 2,
        normed_t, heads_t, over_cores(normed_t), over_cores(heads_t),
        scratch=turn_scratch, cost=LIGHT,
    )
    shares = [((F, ROWS, 128), BF)]
    shares_t = call(
        weight_shares, shares, turned_t, other_t, keep, over_cores(send),
        cost=LIGHT, parts=SHARE_PARTS, pieces=4,
    )[0]
    got, shares_t = lax.optimization_barrier((got, shares_t))
    shares_t = lax.all_to_all(shares_t, "seq", 0, 0, tiled=True)
    dmid, dqkv, keep, send = call(
        spatial_back,
        [((N, D), BF), ((N, PACK), BF)] + halves,
        got, marks, mods, wo_s, v, probs, q, k,
        step=t_index, scratch=[((N, 2 * GO), BF), ((N, W), BF)],
    )
    shares_s = call(
        weight_shares, shares, turned_s, other_s, keep, over_cores(send),
        parts=SHARE_PARTS, pieces=4,
    )[0]
    shares_t, shares_s = lax.optimization_barrier((shares_t, shares_s))
    shares_s = lax.all_to_all(shares_s, "seq", 0, 0, tiled=True)
    grad = call(
        spatial_input, [((N, D), F32)], dqkv, wqkv_s, dmid, x, marks, mods,
        step=t_index, scratch=[((N, D), F32)], cost=LIGHT,
    )[0]
    own_t, grad = lax.optimization_barrier((sum_seq(shares_t), grad))
    one_t, two_t = over_cores(own_t), over_chips(own_t)
    shares_s, one_t, two_t = lax.optimization_barrier((shares_s, one_t, two_t))
    own_s = sum_seq(shares_s)
    two_s = over_chips(own_s)
    shares = [own_t, one_t, two_t, over_cores(two_t), own_s, over_cores(own_s), two_s, over_cores(two_s)]
    results = call(finish, [((36, 3 * HD), F32), ((18, D), F32)] * 2, *shares)
    return (grad[None, None], *results)


def solution(mesh):
    return jax.shard_map(
        body,
        mesh=mesh,
        in_specs=(
            P("dp", "seq", None, None),
            P("dp", "seq", None, None),
            P("dp", None, None),
            P("dp"),
            P(),
            P(),
            P(),
            P(),
            P(),
        ),
        out_specs=(
            P("dp", "seq", None, None),
            P("seq", None),
            P("seq", None),
            P("seq", None),
            P("seq", None),
        ),
        check_vma=False,
    )
```

```python
import math

import jax
import jax.numpy as jnp
from jax import lax
from jax.experimental import pallas as pl
from jax.experimental.pallas import tpu as pltpu
from jax.sharding import PartitionSpec as P

D = 1152
H = 8
E = 72
HD = 576
N = 384
F = 32
W = 640
LATE = 256
REST = 128
PACK = 1792
GQ = 896
GO = 640
ROWS = 352
BF = jnp.bfloat16
F32 = jnp.float32
SCALE = E**-0.5
SMEM = pl.BlockSpec(memory_space=pltpu.SMEM)
ANY = pl.BlockSpec(memory_space=pl.ANY)


class Moves:
    def __init__(self, sems):
        self.sems, self.used, self.coming, self.going = sems, 0, {}, {}

    def copy(self, source, target):
        made = pltpu.make_async_copy(source, target, self.sems.at[self.used])
        self.used += 1
        made.start()
        return made

    def need(self, ref, part=0):
        made = self.coming[id(ref)][part]
        if made is not None:
            made.wait()
            self.coming[id(ref)][part] = None

    def done(self, ref, index=None):
        target, sent = self.going[id(ref)]
        if index is None:
            sent.append(self.copy(ref, target))
        else:
            sent.append(self.copy(ref.at[index], target.at[index]))

    def close(self, ins, outs):
        for ref in ins:
            for part in range(len(self.coming[id(ref)])):
                self.need(ref, part)
        for ref in outs:
            if not self.going[id(ref)][1]:
                self.done(ref)
        for ref in outs:
            for made in self.going[id(ref)][1]:
                made.wait()


def call(kernel, out, *arrays, step=None, scratch=(), cost=None, parts=None, pieces=0):
    count, last = len(arrays), len(arrays) + len(out)
    parts = parts or {}
    cuts = [parts.get(i, [None]) for i in range(count)]
    copies = sum(len(cut) for cut in cuts) + len(out) + pieces
    lead = 0 if step is None else 1

    def whole(*refs):
        scalars, refs = refs[:lead], refs[lead:]
        far, near = refs[:last], refs[last : 2 * last]
        io = Moves(refs[-1])
        for ref, cut in zip(near[:count], cuts):
            io.coming[id(ref)] = [None] * len(cut)
        for step in range(max(len(cut) for cut in cuts)):
            for source, ref, cut in zip(far[:count], near[:count], cuts):
                if step < len(cut):
                    at = cut[step]
                    pair = (source, ref) if at is None else (source.at[at], ref.at[at])
                    io.coming[id(ref)][step] = io.copy(*pair)
        for target, ref in zip(far[count:], near[count:]):
            io.going[id(ref)] = (target, [])
        kernel(io, *scalars, *near, *refs[2 * last : -1])
        io.close(near[:count], near[count:])

    near = [pltpu.VMEM(array.shape, array.dtype) for array in arrays]
    near += [pltpu.VMEM(shape, kind) for shape, kind in out]
    return pl.pallas_call(
        whole,
        out_shape=[jax.ShapeDtypeStruct(shape, kind) for shape, kind in out],
        in_specs=[SMEM] * lead + [ANY] * count,
        out_specs=[ANY] * len(out),
        scratch_shapes=near
        + [pltpu.VMEM(shape, kind) for shape, kind in scratch]
        + [pltpu.SemaphoreType.DMA((copies,))],
        compiler_params=pltpu.CompilerParams(vmem_limit_bytes=(62 * 1024 + 400) * 1024),
        cost_estimate=cost,
        name=kernel.__name__,
    )(*([] if step is None else [step]), *arrays)


LIGHT = pl.CostEstimate(flops=1000, transcendentals=0, bytes_accessed=1000)


def nn(a, b):
    return lax.dot_general(a, b, (((1,), (0,)), ((), ())), preferred_element_type=F32)


def nt(a, b):
    return lax.dot_general(a, b, (((1,), (1,)), ((), ())), preferred_element_type=F32)


def tn(a, b):
    return lax.dot_general(a, b, (((0,), (0,)), ((), ())), preferred_element_type=F32)


def iota(shape, dim):
    return lax.broadcasted_iota(jnp.int32, shape, dim)


def one_hot(test):
    return jnp.where(test, 1.0, 0.0).astype(BF)


def rest_pick(back):
    shape = (LATE, 2 * REST)
    row, col = iota(shape, 0), iota(shape, 1)
    if back:
        shape = (2 * REST, LATE)
        row, col = iota(shape, 1), iota(shape, 0)
    return one_hot((row & 3) + 4 * (row >> 3) + REST * ((row >> 2) & 1) == col)


def pack_frame(rows, out_ref, at):
    out_ref[:, at : at + D] = rows[:LATE]
    low = rows[LATE:, :W]
    high = jnp.concatenate([rows[LATE:, W:], jnp.zeros((REST, 2 * W - D), BF)], axis=1)
    both = jnp.concatenate([low, high], axis=0)
    out_ref[:, at + D : at + PACK] = nn(rest_pick(False), both).astype(BF)


def unpack_frame(got_ref):
    both = nn(rest_pick(True), got_ref[:, D:])
    rest = jnp.concatenate([both[:REST], both[REST:, : D - W]], axis=1).astype(BF)
    return got_ref[:, :D], rest


def patch_pick():
    shape = (LATE, LATE)
    row, col = iota(shape, 0), iota(shape, 1)
    return one_hot((row & 31) * 8 + (row >> 5) == col)


def unpack_patches(got_ref, pick, at):
    first = nn(pick, got_ref[:, at : at + D])
    rest = nn(pick, got_ref[:, at + D : at + PACK])
    rest = jnp.concatenate([rest[:REST], rest[REST:, : D - W]], axis=1)
    return jnp.concatenate([first, rest], axis=0).astype(BF)


def pack_patches(rows, pick, out_ref):
    out_ref[:, :D] = tn(pick, rows[:LATE]).astype(BF)
    low = rows[LATE:, :W]
    high = jnp.concatenate([rows[LATE:, W:], jnp.zeros((REST, 2 * W - D), BF)], axis=1)
    out_ref[:, D:] = tn(pick, jnp.concatenate([low, high], axis=0)).astype(BF)


def head_window(head):
    first = head * E // 128 * 128
    last = -(-(head + 1) * E // 128) * 128
    lane = iota((1, last - first), 1) + first
    keep = one_hot((lane >= head * E) & (lane < (head + 1) * E))
    return slice(first, last), keep


def frame_marks(mask_ref):
    row = mask_ref[pl.ds(lax.axis_index("seq"), 1), :].astype(F32)
    return jnp.transpose(jnp.broadcast_to(row, (128, N)))


def patch_marks(mask_ref):
    rank = lax.axis_index("seq")
    shape = (N, F)
    spread = nn(one_hot((iota(shape, 0) & 31) == iota(shape, 1)), mask_ref[...].astype(F32).astype(BF))
    place = iota((N, N), 0) >> 5
    patch = jnp.where(place < 8, rank * 8 + place, LATE + rank * 4 + place - 8)
    chosen = jnp.where(patch == iota((N, N), 1), spread, 0.0)
    return jnp.broadcast_to(jnp.sum(chosen, axis=1, keepdims=True), (N, 128))


def modulation(mod_ref, step, row, marks, rows):
    clean = mod_ref[row, 0:1, :]
    noised = mod_ref[row, pl.ds(step, 1), :]
    wide = jnp.concatenate([marks[rows]] * (D // 128), axis=1)
    return jnp.where(wide == 1.0, clean, noised)


def chunks(size):
    return [slice(i, i + size) for i in range(0, N, size)]


def normalize(x):
    centered = x - jnp.mean(x, axis=1, keepdims=True)
    inverse = lax.rsqrt(jnp.mean(centered * centered, axis=1, keepdims=True) + 1e-06)
    return centered * inverse, inverse


def project(normed, w_ref, q_ref, k_ref, v_ref):
    for i, ref in enumerate((q_ref, k_ref, v_ref)):
        ref[:, :HD] = nt(normed, w_ref[HD * i : HD * i + HD, :]).astype(BF)
        ref[:, HD:] = jnp.zeros((N, W - HD), BF)


class Blocks:
    def __init__(self):
        self.parts = [[] for _ in range(W // 128)]

    def add(self, lanes, value):
        for i in range((lanes.stop - lanes.start) // 128):
            self.parts[lanes.start // 128 + i].append(value[:, 128 * i : 128 * i + 128])

    def join(self):
        return jnp.concatenate([sum(parts[1:], parts[0]) for parts in self.parts], axis=1)


def batches(groups, batch):
    units = [(i, head, *head_window(head)) for i in range(len(groups)) for head in range(H)]
    return [units[i : i + batch] for i in range(0, len(units), batch)]


def attend(q_ref, k_ref, v_ref, probs_ref, heads_ref, groups, batch, same=None):
    heads = [Blocks() for _ in groups]
    for units in batches(groups, batch):
        scores = []
        for i, _, lanes, keep in units:
            scores.append(nt(k_ref[groups[i], lanes], q_ref[groups[i], lanes] * keep))
        probs = []
        for score in scores:
            if same is not None:
                score = jnp.where(same, score, -1e30)
            top = jnp.max(score, axis=0, keepdims=True)
            expo = jnp.exp2((score - top) * (SCALE * math.log2(math.e)))
            share = 1.0 / jnp.sum(expo, axis=0, keepdims=True)
            probs.append((expo * share).astype(BF))
        for prob, (i, _, lanes, keep) in zip(probs, units):
            heads[i].add(lanes, tn(prob, v_ref[groups[i], lanes] * keep))
        for prob, (i, head, _, _) in zip(probs, units):
            probs_ref[head, groups[i], :] = prob
    for rows, parts in zip(groups, heads):
        heads_ref[rows, :] = parts.join().astype(BF)


def attend_back(q_ref, k_ref, v_ref, probs_ref, dheads_ref, dqkv_ref, groups, batch):
    sums = [(Blocks(), Blocks(), Blocks()) for _ in groups]
    for units in batches(groups, batch):
        dheads = [dheads_ref[groups[i], lanes] * keep for i, _, lanes, keep in units]
        dprobs = []
        for dhead, (i, _, lanes, _) in zip(dheads, units):
            dprobs.append(nt(v_ref[groups[i], lanes], dhead))
        dscores = []
        for dprob, (i, head, _, _) in zip(dprobs, units):
            wide = probs_ref[head, groups[i], :].astype(F32)
            total = jnp.sum(wide * dprob, axis=0, keepdims=True)
            dscores.append((wide * (dprob - total)).astype(BF))
        for dhead, dscore, (i, head, lanes, keep) in zip(dheads, dscores, units):
            dq, dk, dv = sums[i]
            dv.add(lanes, nn(probs_ref[head, groups[i], :], dhead))
            dk.add(lanes, nn(dscore, q_ref[groups[i], lanes] * keep))
            dq.add(lanes, tn(dscore, k_ref[groups[i], lanes] * keep))
    for rows, (dq, dk, dv) in zip(groups, sums):
        query, low = dq.join() * SCALE, pltpu.roll(dk.join() * SCALE, W - HD, 1)
        dqkv_ref[rows, : W - 128] = query[:, : W - 128].astype(BF)
        dqkv_ref[rows, W - 128 : W] = (query[:, W - 128 :] + low[:, :128]).astype(BF)
        dqkv_ref[rows, W : 2 * HD] = low[:, 128:].astype(BF)
        dqkv_ref[rows, 2 * HD :] = dv.join().astype(BF)


def split_halves(io, dqkv_ref, dattn_ref, keep_ref, send_ref):
    core = lax.axis_index("dp") & 1
    for ref, side in ((keep_ref, core), (send_ref, 1 - core)):
        target, sent = io.going[id(ref)]
        for source, width, start in ((dqkv_ref, GQ, 0), (dattn_ref, GO, GQ)):
            lanes = pl.ds(pl.multiple_of(side * width, 128), width)
            sent.append(io.copy(source.at[:, lanes], target.at[:, start : start + width]))


def gated(dout_ref, mod_ref, step, row, marks, dattn_ref):
    for rows in chunks(128):
        gate = modulation(mod_ref, step, row, marks, rows)
        dattn_ref[rows, :D] = (dout_ref[rows, :].astype(F32) * gate).astype(BF)
    dattn_ref[:, D:] = jnp.zeros((N, 2 * GO - D), BF)


def input_gradient(x_ref, dout_ref, dnormed_ref, mod_ref, step, row, marks, out_ref):
    for rows in chunks(128):
        xhat, inverse = normalize(x_ref[rows, :].astype(F32))
        scale = 1.0 + modulation(mod_ref, step, row, marks, rows)
        dxhat = dnormed_ref[rows, :] * scale
        first = jnp.mean(dxhat, axis=1, keepdims=True)
        second = jnp.mean(dxhat * xhat, axis=1, keepdims=True)
        line = inverse * (dxhat - first - xhat * second)
        out_ref[rows, :] = (dout_ref[rows, :].astype(F32) + line).astype(out_ref.dtype)


def norm_rows(x_ref, mod_ref, step, row, marks, normed_ref):
    for rows in chunks(128):
        xhat, _ = normalize(x_ref[rows, :].astype(F32))
        shift = modulation(mod_ref, step, row, marks, rows)
        scale = modulation(mod_ref, step, row + 1, marks, rows)
        normed_ref[rows, :] = (xhat * (1.0 + scale) + shift).astype(BF)


def spatial_forward(
    io, s_ref, x_ref, mask_ref, mod_ref, wqkv_ref, wo_ref, cot_ref,
    packed_ref, normed_ref, q_ref, k_ref, v_ref, probs_ref, heads_ref, mid,
):
    step = s_ref[0]
    io.need(mask_ref)
    marks = frame_marks(mask_ref)
    io.need(x_ref)
    io.need(mod_ref)
    norm_rows(x_ref, mod_ref, step, 0, marks, normed_ref)
    io.done(normed_ref)
    io.need(wqkv_ref)
    project(normed_ref[...], wqkv_ref, q_ref, k_ref, v_ref)
    for ref in (q_ref, k_ref, v_ref):
        io.done(ref)
    attend(q_ref, k_ref, v_ref, probs_ref, heads_ref, [slice(0, N)], 8)
    io.done(probs_ref)
    io.done(heads_ref)
    io.need(cot_ref)
    pack_frame(cot_ref[...], packed_ref, PACK)
    io.need(wo_ref)
    attn = nn(heads_ref[:, :HD], wo_ref[...])
    for rows in chunks(128):
        gate = modulation(mod_ref, step, 2, marks, rows)
        mid[rows, :] = (x_ref[rows, :].astype(F32) + gate * attn[rows]).astype(BF)
    pack_frame(mid[...], packed_ref, 0)


def temporal(
    io, s_ref, got_ref, mask_ref, mod_ref, wqkv_ref, wo_ref,
    packed_ref, normed_ref, heads_ref, keep_ref, send_ref,
    x, dout, q, k, v, probs, dqkv, dattn, dheads, dnormed, dmid,
):
    step = s_ref[0]
    io.need(mask_ref)
    marks = patch_marks(mask_ref)
    pick = patch_pick()
    io.need(got_ref)
    x[...] = unpack_patches(got_ref, pick, 0)
    io.need(mod_ref)
    norm_rows(x, mod_ref, step, 3, marks, normed_ref)
    io.done(normed_ref)
    io.need(wqkv_ref)
    project(normed_ref[...], wqkv_ref, q, k, v)
    groups = chunks(128)
    same = (iota((128, 128), 0) >> 5) == (iota((128, 128), 1) >> 5)
    attend(q, k, v, probs, heads_ref, groups, 3 * H, same)
    io.done(heads_ref)
    dout[...] = unpack_patches(got_ref, pick, PACK)
    gated(dout, mod_ref, step, 5, marks, dattn)
    io.need(wo_ref)
    dheads[:, :HD] = nt(dattn[:, :D], wo_ref[...]).astype(BF)
    dheads[:, HD:] = jnp.zeros((N, W - HD), BF)
    attend_back(q, k, v, probs, dheads, dqkv, groups, 3 * H)
    split_halves(io, dqkv, dattn, keep_ref, send_ref)
    dnormed[...] = nn(dqkv[:, : 3 * HD], wqkv_ref[...])
    input_gradient(x, dout, dnormed, mod_ref, step, 4, marks, dmid)
    pack_patches(dmid[...], pick, packed_ref)


def spatial_back(
    io, s_ref, got_ref, mask_ref, mod_ref, wo_ref, v_ref, probs_ref, q_ref, k_ref,
    dmid_ref, dqkv_ref, keep_ref, send_ref, dattn, dheads,
):
    io.need(mask_ref)
    marks = frame_marks(mask_ref)
    io.need(got_ref)
    first, rest = unpack_frame(got_ref)
    dmid_ref[:LATE, :] = first
    dmid_ref[LATE:, :] = rest
    io.done(dmid_ref)
    io.need(mod_ref)
    gated(dmid_ref, mod_ref, s_ref[0], 2, marks, dattn)
    io.need(wo_ref)
    dheads[:, :HD] = nt(dattn[:, :D], wo_ref[...]).astype(BF)
    dheads[:, HD:] = jnp.zeros((N, W - HD), BF)
    for ref in (v_ref, probs_ref, q_ref, k_ref):
        io.need(ref)
    attend_back(q_ref, k_ref, v_ref, probs_ref, dheads, dqkv_ref, [slice(0, N)], 4)
    io.done(dqkv_ref)
    split_halves(io, dqkv_ref, dattn, keep_ref, send_ref)


def spatial_input(io, s_ref, dqkv_ref, wqkv_ref, dmid_ref, x_ref, mask_ref, mod_ref, out_ref, dnormed):
    io.need(dqkv_ref)
    io.need(wqkv_ref)
    dnormed[...] = nn(dqkv_ref[:, : 3 * HD], wqkv_ref[...])
    for ref in (dmid_ref, x_ref, mask_ref, mod_ref):
        io.need(ref)
    marks = frame_marks(mask_ref)
    input_gradient(x_ref, dmid_ref, dnormed, mod_ref, s_ref[0], 1, marks, out_ref)


def turn(normed_ref, heads_ref, out_ref, wide, tall):
    wide[:D, :] = jnp.transpose(normed_ref[...].astype(F32))
    wide[D:, :] = jnp.zeros((8, N), F32)
    tall[:W, :] = jnp.transpose(heads_ref[...].astype(F32))
    tall[W:, :] = jnp.zeros((8, N), F32)
    place = iota((8, N), 0)
    for i in range(0, F, 2):
        fours, twos = [], []
        for j in (i, i + 1):
            out_ref[32 * j : 32 * j + 32, :] = wide[36 * j : 36 * j + 32, :].astype(BF)
            out_ref[1280 + 16 * j : 1296 + 16 * j, :] = tall[18 * j : 18 * j + 16, :].astype(BF)
            base = 36 * j + 32
            fours.append(jnp.where(place < 4, wide[base : base + 8, :], wide[base - 4 : base + 4, :]))
            base = 18 * j + 16
            two = tall[base : base + 8, :]
            for shift in (2, 4, 6):
                two = jnp.where(place < shift, two, tall[base - shift : base - shift + 8, :])
            twos.append(two)
        out_ref[1024 + 8 * i : 1040 + 8 * i, :] = jnp.concatenate(fours, axis=0).astype(BF)
        out_ref[1792 + 8 * i : 1808 + 8 * i, :] = jnp.concatenate(twos, axis=0).astype(BF)


def turn_spatial(io, normed_ref, heads_ref, out_ref, wide, tall):
    io.need(normed_ref)
    io.need(heads_ref)
    turn(normed_ref, heads_ref, out_ref, wide, tall)


def turn_temporal(
    io, normed_ref, heads_ref, normed_other_ref, heads_other_ref, own_ref, other_ref, wide, tall
):
    io.need(normed_ref)
    io.need(heads_ref)
    turn(normed_ref, heads_ref, own_ref, wide, tall)
    io.done(own_ref)
    io.need(normed_other_ref)
    io.need(heads_other_ref)
    turn(normed_other_ref, heads_other_ref, other_ref, wide, tall)


SHARE_PARTS = {
    0: [(slice(1280, 2048), slice(None)), (slice(0, 1280), slice(None))],
    1: [(slice(1280, 2048), slice(None)), (slice(0, 1280), slice(None))],
    2: [(slice(None), slice(GQ, GQ + GO)), (slice(None), slice(0, GQ))],
    3: [(slice(None), slice(GQ, GQ + GO)), (slice(None), slice(0, GQ))],
}


def weight_shares(io, a_ref, b_ref, keep_ref, got_ref, out_ref):
    def both(rows):
        return jnp.concatenate([a_ref[rows, :], b_ref[rows, :]], axis=1)

    def pair(lanes):
        return jnp.concatenate([keep_ref[:, lanes], got_ref[:, lanes]], axis=0)

    def send(start, size):
        io.done(out_ref, (slice(None), slice(start, start + size), slice(None)))

    place = iota((F * 8, 128), 0) & 7
    for ref in (a_ref, b_ref, keep_ref, got_ref):
        io.need(ref, 0)
    main, rest = both(slice(1280, 1792)), both(slice(1792, 2048))
    right = pair(slice(GQ, GQ + GO))
    part, last = nn(main, right).astype(BF), nn(rest, right)
    for j in range(5):
        out_ref[:, 224 + 16 * j : 240 + 16 * j, :] = part[:, 128 * j : 128 * j + 128].reshape(F, 16, 128)
    four = last[:, :128]
    for j in (1, 2, 3):
        four = jnp.where(place < 2 * j, four, last[:, 128 * j : 128 * j + 128])
    both_extra = [four.reshape(F, 8, 128), last[:, 512:].reshape(F, 8, 128)]
    out_ref[:, 336:352, :] = jnp.concatenate(both_extra, axis=1).astype(BF)
    for ref in (a_ref, b_ref, keep_ref, got_ref):
        io.need(ref, 1)
    main, rest = both(slice(0, 1024)), both(slice(1024, 1280))
    extra = []
    for j in range(0, 7, 2):
        lanes = slice(128 * j, min(128 * j + 256, GQ))
        right = pair(lanes)
        part = nn(main, right).astype(BF)
        out_ref[:, 32 * j : 32 * j + 32, :] = part[:, :128].reshape(F, 32, 128)
        last = nn(rest, right)
        if j < 6:
            out_ref[:, 32 * j + 32 : 32 * j + 64, :] = part[:, 128:].reshape(F, 32, 128)
            last = jnp.where(place < 4, last[:, :128], last[:, 128:])
            send(32 * j, 64)
        extra.append(last.reshape(F, 8, 128))
    for j in range(2):
        both_extra = jnp.concatenate(extra[2 * j : 2 * j + 2], axis=1)
        out_ref[:, 304 + 16 * j : 320 + 16 * j, :] = both_extra.astype(BF)
    send(192, 160)


SUM_STARTS = [0, 80, 160, 256, ROWS]
SUM_PARTS = [(slice(None), slice(i, j), slice(None)) for i, j in zip(SUM_STARTS, SUM_STARTS[1:])]


def sum_shares(io, got_ref, out_ref):
    for part in range(4):
        io.need(got_ref, part)
        for start in range(SUM_STARTS[part], SUM_STARTS[part + 1], 16):
            rows = slice(start, start + 16)
            sums = [got_ref[i, rows, :].astype(F32) for i in range(F)]
            while len(sums) > 1:
                sums = [one + two for one, two in zip(sums[::2], sums[1::2])]
            out_ref[rows, :] = sums[0].astype(BF)


def place_shares(own, one, two, three, q_ref, o_ref):
    factor = 1.0 / math.sqrt(4 * F * N)
    own, one, two, three = (ref[...].astype(F32) for ref in (own, one, two, three))
    same, other = (own + two) * factor, (one + three) * factor
    first = (lax.axis_index("dp") & 1) == 0
    halves = [jnp.where(first, same, other), jnp.where(first, other, same)]
    for side, half in enumerate(halves):
        for j in range(7):
            start = GQ * side + 128 * j
            width = min(128, 3 * HD - start)
            q_ref[:32, start : start + width] = half[32 * j : 32 * j + 32, :width]
            base = 304 + 4 * j
            q_ref[32:, start : start + width] = half[base : base + 4, :width]
        for j in range(5):
            start = GO * side + 128 * j
            if start < D:
                o_ref[:16, start : start + 128] = half[224 + 16 * j : 240 + 16 * j, :]
                o_ref[16:, start : start + 128] = half[336 + 2 * j : 338 + 2 * j, :]


def finish(io, *refs):
    temporal_refs, spatial_refs, outs = refs[:4], refs[4:8], refs[8:]
    for ref in temporal_refs:
        io.need(ref)
    place_shares(*temporal_refs, *outs[2:])
    for ref in outs[2:]:
        io.done(ref)
    for ref in spatial_refs:
        io.need(ref)
    place_shares(*spatial_refs, *outs[:2])


def sum_seq(got):
    return call(sum_shares, [((ROWS, 128), BF)], got, cost=LIGHT, parts={0: SUM_PARTS})[0]


def over_chips(array):
    return lax.ppermute(array, "dp", [(0, 2), (1, 3), (2, 0), (3, 1)])


def over_cores(array):
    return lax.ppermute(array, "dp", [(0, 1), (1, 0), (2, 3), (3, 2)])


def exchange(packed):
    shape = packed.shape
    sent = lax.all_to_all(packed.reshape(F, shape[0] // F, shape[1]), "seq", 0, 0, tiled=True)
    return sent.reshape(shape)


def body(tokens, cotangent, mask, t_index, mod_table, wqkv_s, wo_s, wqkv_t, wo_t):
    x, cot, marks = tokens[0, 0], cotangent[0, 0], mask[0]
    mods, wqkv_s, wqkv_t = jnp.transpose(mod_table, (1, 0, 2)), wqkv_s.T, wqkv_t.T
    packed, normed_s, q, k, v, probs, heads_s = call(
        spatial_forward,
        [((LATE, 2 * PACK), BF), ((N, D), BF)] + [((N, W), BF)] * 3 + [((H, N, N), BF), ((N, W), BF)],
        x, marks, mods, wqkv_s, wo_s, cot,
        step=t_index, scratch=[((N, D), BF)],
    )
    got = exchange(packed)
    turn_scratch = [((D + 8, N), F32), ((W + 8, N), F32)]
    turned = [((2048, N), BF)]
    turned_s = call(turn_spatial, turned, normed_s, heads_s, scratch=turn_scratch, cost=LIGHT)[0]
    other_s = over_cores(turned_s)
    got, turned_s = lax.optimization_barrier((got, turned_s))
    halves = [((N, GQ + GO), BF)] * 2
    packed, normed_t, heads_t, keep, send = call(
        temporal,
        [((LATE, PACK), BF), ((N, D), BF), ((N, W), BF)] + halves,
        got, marks, mods, wqkv_t, wo_t,
        step=t_index, pieces=2, scratch=[((N, D), BF)] * 2 + [((N, W), BF)] * 3 + [((H, N, 128), BF)]
        + [((N, PACK), BF), ((N, 2 * GO), BF), ((N, W), BF), ((N, D), F32), ((N, D), BF)],
    )
    got = exchange(packed)
    turned_t, other_t = call(
        turn_temporal, turned * 2,
        normed_t, heads_t, over_cores(normed_t), over_cores(heads_t),
        scratch=turn_scratch, cost=LIGHT,
    )
    shares = [((F, ROWS, 128), BF)]
    shares_t = call(
        weight_shares, shares, turned_t, other_t, keep, over_cores(send),
        cost=LIGHT, parts=SHARE_PARTS, pieces=4,
    )[0]
    got, shares_t = lax.optimization_barrier((got, shares_t))
    shares_t = lax.all_to_all(shares_t, "seq", 0, 0, tiled=True)
    dmid, dqkv, keep, send = call(
        spatial_back,
        [((N, D), BF), ((N, PACK), BF)] + halves,
        got, marks, mods, wo_s, v, probs, q, k,
        step=t_index, pieces=2, scratch=[((N, 2 * GO), BF), ((N, W), BF)],
    )
    shares_s = call(
        weight_shares, shares, turned_s, other_s, keep, over_cores(send),
        parts=SHARE_PARTS, pieces=4,
    )[0]
    shares_t, shares_s = lax.optimization_barrier((shares_t, shares_s))
    shares_s = lax.all_to_all(shares_s, "seq", 0, 0, tiled=True)
    grad = call(
        spatial_input, [((N, D), F32)], dqkv, wqkv_s, dmid, x, marks, mods,
        step=t_index, scratch=[((N, D), F32)], cost=LIGHT,
    )[0]
    own_t, grad = lax.optimization_barrier((sum_seq(shares_t), grad))
    one_t, two_t = over_cores(own_t), over_chips(own_t)
    shares_s, one_t, two_t = lax.optimization_barrier((shares_s, one_t, two_t))
    own_s = sum_seq(shares_s)
    two_s = over_chips(own_s)
    shares = [own_t, one_t, two_t, over_cores(two_t), own_s, over_cores(own_s), two_s, over_cores(two_s)]
    results = call(finish, [((36, 3 * HD), F32), ((18, D), F32)] * 2, *shares)
    return (grad[None, None], *results)


def solution(mesh):
    return jax.shard_map(
        body,
        mesh=mesh,
        in_specs=(
            P("dp", "seq", None, None),
            P("dp", "seq", None, None),
            P("dp", None, None),
            P("dp"),
            P(),
            P(),
            P(),
            P(),
            P(),
        ),
        out_specs=(
            P("dp", "seq", None, None),
            P("seq", None),
            P("seq", None),
            P("seq", None),
            P("seq", None),
        ),
        check_vma=False,
    )
```

```python
import math

import jax
import jax.numpy as jnp
from jax import lax
from jax.experimental import pallas as pl
from jax.experimental.pallas import tpu as pltpu
from jax.sharding import PartitionSpec as P

D = 1152
H = 8
E = 72
HD = 576
N = 384
F = 32
W = 640
LATE = 256
REST = 128
PACK = 1792
GQ = 896
GO = 640
ROWS = 352
BF = jnp.bfloat16
F32 = jnp.float32
SCALE = E**-0.5
SMEM = pl.BlockSpec(memory_space=pltpu.SMEM)
ANY = pl.BlockSpec(memory_space=pl.ANY)


class Moves:
    def __init__(self, sems):
        self.sems, self.used, self.coming, self.going = sems, 0, {}, {}

    def copy(self, source, target):
        made = pltpu.make_async_copy(source, target, self.sems.at[self.used])
        self.used += 1
        made.start()
        return made

    def need(self, ref, part=0):
        made = self.coming[id(ref)][part]
        if made is not None:
            made.wait()
            self.coming[id(ref)][part] = None

    def done(self, ref, index=None):
        target, sent = self.going[id(ref)]
        if index is None:
            sent.append(self.copy(ref, target))
        else:
            sent.append(self.copy(ref.at[index], target.at[index]))

    def close(self, ins, outs):
        for ref in ins:
            for part in range(len(self.coming[id(ref)])):
                self.need(ref, part)
        for ref in outs:
            if not self.going[id(ref)][1]:
                self.done(ref)
        for ref in outs:
            for made in self.going[id(ref)][1]:
                made.wait()


def call(kernel, out, *arrays, step=None, scratch=(), cost=None, parts=None, pieces=0):
    count, last = len(arrays), len(arrays) + len(out)
    parts = parts or {}
    cuts = [parts.get(i, [None]) for i in range(count)]
    copies = sum(len(cut) for cut in cuts) + len(out) + pieces
    lead = 0 if step is None else 1

    def whole(*refs):
        scalars, refs = refs[:lead], refs[lead:]
        far, near = refs[:last], refs[last : 2 * last]
        io = Moves(refs[-1])
        for ref, cut in zip(near[:count], cuts):
            io.coming[id(ref)] = [None] * len(cut)
        for step in range(max(len(cut) for cut in cuts)):
            for source, ref, cut in zip(far[:count], near[:count], cuts):
                if step < len(cut):
                    at = cut[step]
                    pair = (source, ref) if at is None else (source.at[at], ref.at[at])
                    io.coming[id(ref)][step] = io.copy(*pair)
        for target, ref in zip(far[count:], near[count:]):
            io.going[id(ref)] = (target, [])
        kernel(io, *scalars, *near, *refs[2 * last : -1])
        io.close(near[:count], near[count:])

    near = [pltpu.VMEM(array.shape, array.dtype) for array in arrays]
    near += [pltpu.VMEM(shape, kind) for shape, kind in out]
    return pl.pallas_call(
        whole,
        out_shape=[jax.ShapeDtypeStruct(shape, kind) for shape, kind in out],
        in_specs=[SMEM] * lead + [ANY] * count,
        out_specs=[ANY] * len(out),
        scratch_shapes=near
        + [pltpu.VMEM(shape, kind) for shape, kind in scratch]
        + [pltpu.SemaphoreType.DMA((copies,))],
        compiler_params=pltpu.CompilerParams(vmem_limit_bytes=(62 * 1024 + 400) * 1024),
        cost_estimate=cost,
        name=kernel.__name__,
    )(*([] if step is None else [step]), *arrays)


LIGHT = pl.CostEstimate(flops=1000, transcendentals=0, bytes_accessed=1000)


def nn(a, b):
    return lax.dot_general(a, b, (((1,), (0,)), ((), ())), preferred_element_type=F32)


def nt(a, b):
    return lax.dot_general(a, b, (((1,), (1,)), ((), ())), preferred_element_type=F32)


def tn(a, b):
    return lax.dot_general(a, b, (((0,), (0,)), ((), ())), preferred_element_type=F32)


def iota(shape, dim):
    return lax.broadcasted_iota(jnp.int32, shape, dim)


def one_hot(test):
    return jnp.where(test, 1.0, 0.0).astype(BF)


def rest_pick(back):
    shape = (LATE, 2 * REST)
    row, col = iota(shape, 0), iota(shape, 1)
    if back:
        shape = (2 * REST, LATE)
        row, col = iota(shape, 1), iota(shape, 0)
    return one_hot((row & 3) + 4 * (row >> 3) + REST * ((row >> 2) & 1) == col)


def pack_frame(rows, out_ref, at):
    out_ref[:, at : at + D] = rows[:LATE]
    low = rows[LATE:, :W]
    high = jnp.concatenate([rows[LATE:, W:], jnp.zeros((REST, 2 * W - D), BF)], axis=1)
    both = jnp.concatenate([low, high], axis=0)
    out_ref[:, at + D : at + PACK] = nn(rest_pick(False), both).astype(BF)


def unpack_frame(got_ref):
    both = nn(rest_pick(True), got_ref[:, D:])
    rest = jnp.concatenate([both[:REST], both[REST:, : D - W]], axis=1).astype(BF)
    return got_ref[:, :D], rest


def patch_pick():
    shape = (LATE, LATE)
    row, col = iota(shape, 0), iota(shape, 1)
    return one_hot((row & 31) * 8 + (row >> 5) == col)


def unpack_patches(got_ref, pick, at):
    first = nn(pick, got_ref[:, at : at + D])
    rest = nn(pick, got_ref[:, at + D : at + PACK])
    rest = jnp.concatenate([rest[:REST], rest[REST:, : D - W]], axis=1)
    return jnp.concatenate([first, rest], axis=0).astype(BF)


def pack_patches(rows, pick, out_ref):
    out_ref[:, :D] = tn(pick, rows[:LATE]).astype(BF)
    low = rows[LATE:, :W]
    high = jnp.concatenate([rows[LATE:, W:], jnp.zeros((REST, 2 * W - D), BF)], axis=1)
    out_ref[:, D:] = tn(pick, jnp.concatenate([low, high], axis=0)).astype(BF)


def head_window(head):
    first = head * E // 128 * 128
    last = -(-(head + 1) * E // 128) * 128
    lane = iota((1, last - first), 1) + first
    keep = one_hot((lane >= head * E) & (lane < (head + 1) * E))
    return slice(first, last), keep


def frame_marks(mask_ref):
    row = mask_ref[pl.ds(lax.axis_index("seq"), 1), :].astype(F32)
    return jnp.transpose(jnp.broadcast_to(row, (128, N)))


def patch_marks(mask_ref):
    rank = lax.axis_index("seq")
    shape = (N, F)
    spread = nn(one_hot((iota(shape, 0) & 31) == iota(shape, 1)), mask_ref[...].astype(F32).astype(BF))
    place = iota((N, N), 0) >> 5
    patch = jnp.where(place < 8, rank * 8 + place, LATE + rank * 4 + place - 8)
    chosen = jnp.where(patch == iota((N, N), 1), spread, 0.0)
    return jnp.broadcast_to(jnp.sum(chosen, axis=1, keepdims=True), (N, 128))


def modulation(mod_ref, step, row, marks, rows):
    clean = mod_ref[row, 0:1, :]
    noised = mod_ref[row, pl.ds(step, 1), :]
    wide = jnp.concatenate([marks[rows]] * (D // 128), axis=1)
    return jnp.where(wide == 1.0, clean, noised)


def chunks(size):
    return [slice(i, i + size) for i in range(0, N, size)]


def normalize(x):
    centered = x - jnp.mean(x, axis=1, keepdims=True)
    inverse = lax.rsqrt(jnp.mean(centered * centered, axis=1, keepdims=True) + 1e-06)
    return centered * inverse, inverse


def project(normed, w_ref, q_ref, k_ref, v_ref):
    for i, ref in enumerate((q_ref, k_ref, v_ref)):
        ref[:, :HD] = nt(normed, w_ref[HD * i : HD * i + HD, :]).astype(BF)
        ref[:, HD:] = jnp.zeros((N, W - HD), BF)


class Blocks:
    def __init__(self):
        self.parts = [[] for _ in range(W // 128)]

    def add(self, lanes, value):
        for i in range((lanes.stop - lanes.start) // 128):
            self.parts[lanes.start // 128 + i].append(value[:, 128 * i : 128 * i + 128])

    def join(self):
        return jnp.concatenate([sum(parts[1:], parts[0]) for parts in self.parts], axis=1)


def batches(groups, batch):
    units = [(i, head, *head_window(head)) for i in range(len(groups)) for head in range(H)]
    return [units[i : i + batch] for i in range(0, len(units), batch)]


def attend(q_ref, k_ref, v_ref, probs_ref, heads_ref, groups, batch, same=None):
    heads = [Blocks() for _ in groups]
    for units in batches(groups, batch):
        scores = []
        for i, _, lanes, keep in units:
            scores.append(nt(k_ref[groups[i], lanes], q_ref[groups[i], lanes] * keep))
        probs = []
        for score in scores:
            if same is not None:
                score = jnp.where(same, score, -1e30)
            top = jnp.max(score, axis=0, keepdims=True)
            expo = jnp.exp2((score - top) * (SCALE * math.log2(math.e)))
            share = 1.0 / jnp.sum(expo, axis=0, keepdims=True)
            probs.append((expo * share).astype(BF))
        for prob, (i, _, lanes, keep) in zip(probs, units):
            heads[i].add(lanes, tn(prob, v_ref[groups[i], lanes] * keep))
        for prob, (i, head, _, _) in zip(probs, units):
            probs_ref[head, groups[i], :] = prob
    for rows, parts in zip(groups, heads):
        heads_ref[rows, :] = parts.join().astype(BF)


def attend_back(q_ref, k_ref, v_ref, probs_ref, dheads_ref, dqkv_ref, groups, batch):
    sums = [(Blocks(), Blocks(), Blocks()) for _ in groups]
    for units in batches(groups, batch):
        dheads = [dheads_ref[groups[i], lanes] * keep for i, _, lanes, keep in units]
        dprobs = []
        for dhead, (i, _, lanes, _) in zip(dheads, units):
            dprobs.append(nt(v_ref[groups[i], lanes], dhead))
        dscores = []
        for dprob, (i, head, _, _) in zip(dprobs, units):
            wide = probs_ref[head, groups[i], :].astype(F32)
            total = jnp.sum(wide * dprob, axis=0, keepdims=True)
            dscores.append((wide * (dprob - total)).astype(BF))
        for dhead, dscore, (i, head, lanes, keep) in zip(dheads, dscores, units):
            dq, dk, dv = sums[i]
            dv.add(lanes, nn(probs_ref[head, groups[i], :], dhead))
            dk.add(lanes, nn(dscore, q_ref[groups[i], lanes] * keep))
            dq.add(lanes, tn(dscore, k_ref[groups[i], lanes] * keep))
    for rows, (dq, dk, dv) in zip(groups, sums):
        query, low = dq.join() * SCALE, pltpu.roll(dk.join() * SCALE, W - HD, 1)
        dqkv_ref[rows, : W - 128] = query[:, : W - 128].astype(BF)
        dqkv_ref[rows, W - 128 : W] = (query[:, W - 128 :] + low[:, :128]).astype(BF)
        dqkv_ref[rows, W : 2 * HD] = low[:, 128:].astype(BF)
        dqkv_ref[rows, 2 * HD :] = dv.join().astype(BF)


def split_halves(io, dqkv_ref, dattn_ref, keep_ref, send_ref):
    core = lax.axis_index("dp") & 1
    for ref, side in ((keep_ref, core), (send_ref, 1 - core)):
        target, sent = io.going[id(ref)]
        for source, width, start in ((dqkv_ref, GQ, 0), (dattn_ref, GO, GQ)):
            lanes = pl.ds(pl.multiple_of(side * width, 128), width)
            sent.append(io.copy(source.at[:, lanes], target.at[:, start : start + width]))


def gated(dout_ref, mod_ref, step, row, marks, dattn_ref):
    for rows in chunks(128):
        gate = modulation(mod_ref, step, row, marks, rows)
        dattn_ref[rows, :D] = (dout_ref[rows, :].astype(F32) * gate).astype(BF)
    dattn_ref[:, D:] = jnp.zeros((N, 2 * GO - D), BF)


def input_gradient(x_ref, dout_ref, dnormed_ref, mod_ref, step, row, marks, out_ref):
    for rows in chunks(128):
        xhat, inverse = normalize(x_ref[rows, :].astype(F32))
        scale = 1.0 + modulation(mod_ref, step, row, marks, rows)
        dxhat = dnormed_ref[rows, :] * scale
        first = jnp.mean(dxhat, axis=1, keepdims=True)
        second = jnp.mean(dxhat * xhat, axis=1, keepdims=True)
        line = inverse * (dxhat - first - xhat * second)
        out_ref[rows, :] = (dout_ref[rows, :].astype(F32) + line).astype(out_ref.dtype)


def norm_rows(x_ref, mod_ref, step, row, marks, normed_ref):
    for rows in chunks(128):
        xhat, _ = normalize(x_ref[rows, :].astype(F32))
        shift = modulation(mod_ref, step, row, marks, rows)
        scale = modulation(mod_ref, step, row + 1, marks, rows)
        normed_ref[rows, :] = (xhat * (1.0 + scale) + shift).astype(BF)


def spatial_forward(
    io, s_ref, x_ref, mask_ref, mod_ref, wqkv_ref, wo_ref, cot_ref,
    packed_ref, normed_ref, q_ref, k_ref, v_ref, probs_ref, heads_ref, mid,
):
    step = s_ref[0]
    io.need(mask_ref)
    marks = frame_marks(mask_ref)
    io.need(x_ref)
    io.need(mod_ref)
    norm_rows(x_ref, mod_ref, step, 0, marks, normed_ref)
    io.done(normed_ref)
    io.need(wqkv_ref)
    project(normed_ref[...], wqkv_ref, q_ref, k_ref, v_ref)
    for ref in (q_ref, k_ref, v_ref):
        io.done(ref)
    attend(q_ref, k_ref, v_ref, probs_ref, heads_ref, [slice(0, N)], 8)
    io.done(probs_ref)
    io.done(heads_ref)
    io.need(cot_ref)
    pack_frame(cot_ref[...], packed_ref, PACK)
    io.need(wo_ref)
    attn = nn(heads_ref[:, :HD], wo_ref[...])
    for rows in chunks(128):
        gate = modulation(mod_ref, step, 2, marks, rows)
        mid[rows, :] = (x_ref[rows, :].astype(F32) + gate * attn[rows]).astype(BF)
    pack_frame(mid[...], packed_ref, 0)


GOT_PARTS = {0: [(slice(None), slice(0, PACK)), (slice(None), slice(PACK, 2 * PACK))]}


def temporal(
    io, s_ref, got_ref, mask_ref, mod_ref, wqkv_ref, wo_ref,
    packed_ref, normed_ref, heads_ref, keep_ref, send_ref,
    x, dout, q, k, v, probs, dqkv, dattn, dheads, dnormed, dmid,
):
    step = s_ref[0]
    io.need(mask_ref)
    marks = patch_marks(mask_ref)
    pick = patch_pick()
    io.need(got_ref)
    x[...] = unpack_patches(got_ref, pick, 0)
    io.need(mod_ref)
    norm_rows(x, mod_ref, step, 3, marks, normed_ref)
    io.done(normed_ref)
    io.need(wqkv_ref)
    project(normed_ref[...], wqkv_ref, q, k, v)
    groups = chunks(128)
    same = (iota((128, 128), 0) >> 5) == (iota((128, 128), 1) >> 5)
    attend(q, k, v, probs, heads_ref, groups, 3 * H, same)
    io.done(heads_ref)
    io.need(got_ref, 1)
    dout[...] = unpack_patches(got_ref, pick, PACK)
    gated(dout, mod_ref, step, 5, marks, dattn)
    io.need(wo_ref)
    dheads[:, :HD] = nt(dattn[:, :D], wo_ref[...]).astype(BF)
    dheads[:, HD:] = jnp.zeros((N, W - HD), BF)
    attend_back(q, k, v, probs, dheads, dqkv, groups, 3 * H)
    split_halves(io, dqkv, dattn, keep_ref, send_ref)
    dnormed[...] = nn(dqkv[:, : 3 * HD], wqkv_ref[...])
    input_gradient(x, dout, dnormed, mod_ref, step, 4, marks, dmid)
    pack_patches(dmid[...], pick, packed_ref)


def spatial_back(
    io, s_ref, got_ref, mask_ref, mod_ref, wo_ref, v_ref, probs_ref, q_ref, k_ref,
    dmid_ref, dqkv_ref, keep_ref, send_ref, dattn, dheads,
):
    io.need(mask_ref)
    marks = frame_marks(mask_ref)
    io.need(got_ref)
    first, rest = unpack_frame(got_ref)
    dmid_ref[:LATE, :] = first
    dmid_ref[LATE:, :] = rest
    io.done(dmid_ref)
    io.need(mod_ref)
    gated(dmid_ref, mod_ref, s_ref[0], 2, marks, dattn)
    io.need(wo_ref)
    dheads[:, :HD] = nt(dattn[:, :D], wo_ref[...]).astype(BF)
    dheads[:, HD:] = jnp.zeros((N, W - HD), BF)
    for ref in (v_ref, probs_ref, q_ref, k_ref):
        io.need(ref)
    attend_back(q_ref, k_ref, v_ref, probs_ref, dheads, dqkv_ref, [slice(0, N)], 4)
    io.done(dqkv_ref)
    split_halves(io, dqkv_ref, dattn, keep_ref, send_ref)


def spatial_input(io, s_ref, dqkv_ref, wqkv_ref, dmid_ref, x_ref, mask_ref, mod_ref, out_ref, dnormed):
    io.need(dqkv_ref)
    io.need(wqkv_ref)
    dnormed[...] = nn(dqkv_ref[:, : 3 * HD], wqkv_ref[...])
    for ref in (dmid_ref, x_ref, mask_ref, mod_ref):
        io.need(ref)
    marks = frame_marks(mask_ref)
    input_gradient(x_ref, dmid_ref, dnormed, mod_ref, s_ref[0], 1, marks, out_ref)


def turn(normed_ref, heads_ref, out_ref, wide, tall):
    wide[:D, :] = jnp.transpose(normed_ref[...].astype(F32))
    wide[D:, :] = jnp.zeros((8, N), F32)
    tall[:W, :] = jnp.transpose(heads_ref[...].astype(F32))
    tall[W:, :] = jnp.zeros((8, N), F32)
    place = iota((8, N), 0)
    for i in range(0, F, 2):
        fours, twos = [], []
        for j in (i, i + 1):
            out_ref[32 * j : 32 * j + 32, :] = wide[36 * j : 36 * j + 32, :].astype(BF)
            out_ref[1280 + 16 * j : 1296 + 16 * j, :] = tall[18 * j : 18 * j + 16, :].astype(BF)
            base = 36 * j + 32
            fours.append(jnp.where(place < 4, wide[base : base + 8, :], wide[base - 4 : base + 4, :]))
            base = 18 * j + 16
            two = tall[base : base + 8, :]
            for shift in (2, 4, 6):
                two = jnp.where(place < shift, two, tall[base - shift : base - shift + 8, :])
            twos.append(two)
        out_ref[1024 + 8 * i : 1040 + 8 * i, :] = jnp.concatenate(fours, axis=0).astype(BF)
        out_ref[1792 + 8 * i : 1808 + 8 * i, :] = jnp.concatenate(twos, axis=0).astype(BF)


def turn_spatial(io, normed_ref, heads_ref, out_ref, wide, tall):
    io.need(normed_ref)
    io.need(heads_ref)
    turn(normed_ref, heads_ref, out_ref, wide, tall)


def turn_temporal(
    io, normed_ref, heads_ref, normed_other_ref, heads_other_ref, own_ref, other_ref, wide, tall
):
    io.need(normed_ref)
    io.need(heads_ref)
    turn(normed_ref, heads_ref, own_ref, wide, tall)
    io.done(own_ref)
    io.need(normed_other_ref)
    io.need(heads_other_ref)
    turn(normed_other_ref, heads_other_ref, other_ref, wide, tall)


SHARE_PARTS = {
    0: [(slice(1280, 2048), slice(None)), (slice(0, 1280), slice(None))],
    1: [(slice(1280, 2048), slice(None)), (slice(0, 1280), slice(None))],
    2: [(slice(None), slice(GQ, GQ + GO)), (slice(None), slice(0, GQ))],
    3: [(slice(None), slice(GQ, GQ + GO)), (slice(None), slice(0, GQ))],
}


def weight_shares(io, a_ref, b_ref, keep_ref, got_ref, out_ref):
    def both(rows):
        return jnp.concatenate([a_ref[rows, :], b_ref[rows, :]], axis=1)

    def pair(lanes):
        return jnp.concatenate([keep_ref[:, lanes], got_ref[:, lanes]], axis=0)

    def send(start, size):
        io.done(out_ref, (slice(None), slice(start, start + size), slice(None)))

    place = iota((F * 8, 128), 0) & 7
    for ref in (a_ref, b_ref, keep_ref, got_ref):
        io.need(ref, 0)
    main, rest = both(slice(1280, 1792)), both(slice(1792, 2048))
    right = pair(slice(GQ, GQ + GO))
    part, last = nn(main, right).astype(BF), nn(rest, right)
    for j in range(5):
        out_ref[:, 224 + 16 * j : 240 + 16 * j, :] = part[:, 128 * j : 128 * j + 128].reshape(F, 16, 128)
    four = last[:, :128]
    for j in (1, 2, 3):
        four = jnp.where(place < 2 * j, four, last[:, 128 * j : 128 * j + 128])
    both_extra = [four.reshape(F, 8, 128), last[:, 512:].reshape(F, 8, 128)]
    out_ref[:, 336:352, :] = jnp.concatenate(both_extra, axis=1).astype(BF)
    for ref in (a_ref, b_ref, keep_ref, got_ref):
        io.need(ref, 1)
    main, rest = both(slice(0, 1024)), both(slice(1024, 1280))
    extra = []
    for j in range(0, 7, 2):
        lanes = slice(128 * j, min(128 * j + 256, GQ))
        right = pair(lanes)
        part = nn(main, right).astype(BF)
        out_ref[:, 32 * j : 32 * j + 32, :] = part[:, :128].reshape(F, 32, 128)
        last = nn(rest, right)
        if j < 6:
            out_ref[:, 32 * j + 32 : 32 * j + 64, :] = part[:, 128:].reshape(F, 32, 128)
            last = jnp.where(place < 4, last[:, :128], last[:, 128:])
            send(32 * j, 64)
        extra.append(last.reshape(F, 8, 128))
    for j in range(2):
        both_extra = jnp.concatenate(extra[2 * j : 2 * j + 2], axis=1)
        out_ref[:, 304 + 16 * j : 320 + 16 * j, :] = both_extra.astype(BF)
    send(192, 160)


SUM_STARTS = [0, 80, 160, 256, ROWS]
SUM_PARTS = [(slice(None), slice(i, j), slice(None)) for i, j in zip(SUM_STARTS, SUM_STARTS[1:])]


def sum_shares(io, got_ref, out_ref):
    for part in range(4):
        io.need(got_ref, part)
        for start in range(SUM_STARTS[part], SUM_STARTS[part + 1], 16):
            rows = slice(start, start + 16)
            sums = [got_ref[i, rows, :].astype(F32) for i in range(F)]
            while len(sums) > 1:
                sums = [one + two for one, two in zip(sums[::2], sums[1::2])]
            out_ref[rows, :] = sums[0].astype(BF)


def place_shares(own, one, two, three, q_ref, o_ref):
    factor = 1.0 / math.sqrt(4 * F * N)
    own, one, two, three = (ref[...].astype(F32) for ref in (own, one, two, three))
    same, other = (own + two) * factor, (one + three) * factor
    first = (lax.axis_index("dp") & 1) == 0
    halves = [jnp.where(first, same, other), jnp.where(first, other, same)]
    for side, half in enumerate(halves):
        for j in range(7):
            start = GQ * side + 128 * j
            width = min(128, 3 * HD - start)
            q_ref[:32, start : start + width] = half[32 * j : 32 * j + 32, :width]
            base = 304 + 4 * j
            q_ref[32:, start : start + width] = half[base : base + 4, :width]
        for j in range(5):
            start = GO * side + 128 * j
            if start < D:
                o_ref[:16, start : start + 128] = half[224 + 16 * j : 240 + 16 * j, :]
                o_ref[16:, start : start + 128] = half[336 + 2 * j : 338 + 2 * j, :]


def finish(io, *refs):
    temporal_refs, spatial_refs, outs = refs[:4], refs[4:8], refs[8:]
    for ref in temporal_refs:
        io.need(ref)
    place_shares(*temporal_refs, *outs[2:])
    for ref in outs[2:]:
        io.done(ref)
    for ref in spatial_refs:
        io.need(ref)
    place_shares(*spatial_refs, *outs[:2])


def sum_seq(got):
    return call(sum_shares, [((ROWS, 128), BF)], got, cost=LIGHT, parts={0: SUM_PARTS})[0]


def over_chips(array):
    return lax.ppermute(array, "dp", [(0, 2), (1, 3), (2, 0), (3, 1)])


def over_cores(array):
    return lax.ppermute(array, "dp", [(0, 1), (1, 0), (2, 3), (3, 2)])


def exchange(packed):
    shape = packed.shape
    sent = lax.all_to_all(packed.reshape(F, shape[0] // F, shape[1]), "seq", 0, 0, tiled=True)
    return sent.reshape(shape)


def body(tokens, cotangent, mask, t_index, mod_table, wqkv_s, wo_s, wqkv_t, wo_t):
    x, cot, marks = tokens[0, 0], cotangent[0, 0], mask[0]
    mods, wqkv_s, wqkv_t = jnp.transpose(mod_table, (1, 0, 2)), wqkv_s.T, wqkv_t.T
    packed, normed_s, q, k, v, probs, heads_s = call(
        spatial_forward,
        [((LATE, 2 * PACK), BF), ((N, D), BF)] + [((N, W), BF)] * 3 + [((H, N, N), BF), ((N, W), BF)],
        x, marks, mods, wqkv_s, wo_s, cot,
        step=t_index, scratch=[((N, D), BF)],
    )
    got = exchange(packed)
    turn_scratch = [((D + 8, N), F32), ((W + 8, N), F32)]
    turned = [((2048, N), BF)]
    turned_s = call(turn_spatial, turned, normed_s, heads_s, scratch=turn_scratch, cost=LIGHT)[0]
    other_s = over_cores(turned_s)
    got, turned_s = lax.optimization_barrier((got, turned_s))
    halves = [((N, GQ + GO), BF)] * 2
    packed, normed_t, heads_t, keep, send = call(
        temporal,
        [((LATE, PACK), BF), ((N, D), BF), ((N, W), BF)] + halves,
        got, marks, mods, wqkv_t, wo_t,
        step=t_index, pieces=2, parts=GOT_PARTS, scratch=[((N, D), BF)] * 2 + [((N, W), BF)] * 3 + [((H, N, 128), BF)]
        + [((N, PACK), BF), ((N, 2 * GO), BF), ((N, W), BF), ((N, D), F32), ((N, D), BF)],
    )
    got = exchange(packed)
    turned_t, other_t = call(
        turn_temporal, turned * 2,
        normed_t, heads_t, over_cores(normed_t), over_cores(heads_t),
        scratch=turn_scratch, cost=LIGHT,
    )
    shares = [((F, ROWS, 128), BF)]
    shares_t = call(
        weight_shares, shares, turned_t, other_t, keep, over_cores(send),
        cost=LIGHT, parts=SHARE_PARTS, pieces=4,
    )[0]
    got, shares_t = lax.optimization_barrier((got, shares_t))
    shares_t = lax.all_to_all(shares_t, "seq", 0, 0, tiled=True)
    dmid, dqkv, keep, send = call(
        spatial_back,
        [((N, D), BF), ((N, PACK), BF)] + halves,
        got, marks, mods, wo_s, v, probs, q, k,
        step=t_index, pieces=2, scratch=[((N, 2 * GO), BF), ((N, W), BF)],
    )
    shares_s = call(
        weight_shares, shares, turned_s, other_s, keep, over_cores(send),
        parts=SHARE_PARTS, pieces=4,
    )[0]
    shares_t, shares_s = lax.optimization_barrier((shares_t, shares_s))
    shares_s = lax.all_to_all(shares_s, "seq", 0, 0, tiled=True)
    grad = call(
        spatial_input, [((N, D), F32)], dqkv, wqkv_s, dmid, x, marks, mods,
        step=t_index, scratch=[((N, D), F32)], cost=LIGHT,
    )[0]
    own_t, grad = lax.optimization_barrier((sum_seq(shares_t), grad))
    one_t, two_t = over_cores(own_t), over_chips(own_t)
    shares_s, one_t, two_t = lax.optimization_barrier((shares_s, one_t, two_t))
    own_s = sum_seq(shares_s)
    two_s = over_chips(own_s)
    shares = [own_t, one_t, two_t, over_cores(two_t), own_s, over_cores(own_s), two_s, over_cores(two_s)]
    results = call(finish, [((36, 3 * HD), F32), ((18, D), F32)] * 2, *shares)
    return (grad[None, None], *results)


def solution(mesh):
    return jax.shard_map(
        body,
        mesh=mesh,
        in_specs=(
            P("dp", "seq", None, None),
            P("dp", "seq", None, None),
            P("dp", None, None),
            P("dp"),
            P(),
            P(),
            P(),
            P(),
            P(),
        ),
        out_specs=(
            P("dp", "seq", None, None),
            P("seq", None),
            P("seq", None),
            P("seq", None),
            P("seq", None),
        ),
        check_vma=False,
    )
```
